32 devices in a mesh: view: 2 (over y), scene: 16 (over z, x, core).
Axes of the slice: x: 2, y: 2, z: 4, core: 2. Of those that a mesh axis runs over, the one named last changes fastest.
Arguments:
- means: float32 [64, 3, 128], P(('view', 'scene')), may hold values from -3 to 3
- log_scales: float32 [64, 3, 128], P(('view', 'scene')), may hold values from -3.3 to -0.4, as said below
- rotations: float32 [64, 4, 128], P(('view', 'scene')), may hold values from -2.5 to 2.5
- opacity_logits: float32 [64, 1, 128], P(('view', 'scene')), may hold values from -3 to 3
- colour_coefs: float32 [64, 48, 128], P(('view', 'scene')), may hold values from -2 to 2
- cameras: float32 [2, 16], replicated, may hold values from -1 to 2048, as said below
- exposure: float32 [2, 12], P('view'), may hold values from -1 to 1
- target: float32 [2, 256, 3, 256], P('view', 'scene'), may hold values from 0 to 1
- tile_ids: int32 [2, 256], P('view', 'scene'), may hold values from 0 to 255, each once within a row
- send_list: int32 [2, 16, 16, 2], P('view', 'scene'), may hold values from -1 to 3, as said below
- pair_slots: int32 [2, 256, 4], P('view', 'scene'), may hold values from -1 to 31, as said below
Outputs:
- shown: float32 [2, 256, 3, 256], P('view', 'scene')
- grad_means: float32 [64, 3, 128], P(('view', 'scene'))
- grad_log_scales: float32 [64, 3, 128], P(('view', 'scene'))
- grad_rotations: float32 [64, 4, 128], P(('view', 'scene'))
- grad_opacity: float32 [64, 1, 128], P(('view', 'scene'))
- grad_colour: float32 [64, 48, 128], P(('view', 'scene'))
- grad_exposure: float32 [2, 12], P('view')
The draws below stay inside these ranges and needn't reach their ends.
Inputs may be any that keep to these rules, and one draw needn't show every extreme that they name: send_list[v, s, r, c] is a local block number of owner s or -1; in each row of 2 the live entries come first and are all different, and a row may have none; in every image some renderer gets 2 blocks from every owner. pair_slots[v, t, k] is -1 or s * 2 + c with c below the number of live entries of send_list[v, s, t // 16]; a tile's live entries come first, at least one, all different; in every image each renderer has a tile with 4 live entries. `cameras`: each row is a rotation matrix, a translation, two focal lengths and a principal point; every Gaussian lies at depth 4 or more before each camera. `log_scales`: logarithms of lengths in world units.
All inputs are finite; a program needn't handle non-finite values.
Results may differ from the reference program's by a relative error of at most 0.0003.
Values sent between devices are 32-bit elements; how exact they have to be, the bound alone decides.
A program may use at most 64 MiB of HBM per device.

```python
import jax
import jax.numpy as jnp
from jax import lax

G = 128
PIX = 256
KMAX = 4
CAP = 2
TILE_COLS = 32
BLK_DEV = 2
TILES_DEV = 16
BLOCKS = 64
TILES = 256
N_VIEW = 2
N_SCENE = 16


def routing(key):
    keys = [jax.random.fold_in(key, 11 + step_at) for step_at in range(6)]
    pick_total = TILES_DEV * KMAX
    owner_scores = jax.random.randint(keys[0], (N_VIEW, N_SCENE, TILES_DEV, N_SCENE), 0, 1 << 20) * N_SCENE + jnp.arange(N_SCENE, dtype=jnp.int32)
    owners = lax.top_k(owner_scores, KMAX)[1].astype(jnp.int32)
    tile_count = jax.random.randint(keys[1], (N_VIEW, N_SCENE, TILES_DEV), 1, KMAX + 1)
    full_tile = jax.random.randint(keys[2], (N_VIEW, N_SCENE), 0, TILES_DEV)
    tile_count = jnp.where(jnp.arange(TILES_DEV)[None, None, :] == full_tile[:, :, None], KMAX, tile_count)
    live_pick = (jnp.arange(KMAX)[None, None, None, :] < tile_count[..., None]).reshape(N_VIEW, N_SCENE, pick_total)
    flat_owner = owners.reshape(N_VIEW, N_SCENE, pick_total)
    same_owner = (flat_owner[..., :, None] == flat_owner[..., None, :]) & live_pick[..., :, None]
    pick_index = jnp.arange(pick_total)
    earlier = pick_index[:, None] < pick_index[None, :]
    occurrence = jnp.sum((same_owner & earlier[None, None]).astype(jnp.int32), axis=-2)
    place = occurrence % CAP
    owner_hits = jnp.sum(((flat_owner[..., None] == jnp.arange(N_SCENE)[None, None, None, :]) & live_pick[..., None]).astype(jnp.int32), axis=-2)
    counts = jnp.minimum(owner_hits, CAP)
    hot = jax.random.randint(keys[3], (N_VIEW,), 0, N_SCENE)
    counts = jnp.where(jnp.arange(N_SCENE)[None, :, None] == hot[:, None, None], CAP, counts)
    counts = jnp.transpose(counts, (0, 2, 1))
    owned_count = BLK_DEV * N_VIEW
    scores = jax.random.randint(keys[4], (N_VIEW, N_SCENE, N_SCENE, owned_count), 0, 1 << 20) * owned_count + jnp.arange(owned_count)
    order = jnp.argsort(scores, axis=-1)[..., :CAP].astype(jnp.int32)
    live_send = jnp.arange(CAP)[None, None, None, :] < counts[..., None]
    send = jnp.where(live_send, order, -1).astype(jnp.int32)
    pairs = jnp.where(live_pick, flat_owner * CAP + place, -1)
    return (send, pairs.reshape(N_VIEW, N_SCENE * TILES_DEV, KMAX).astype(jnp.int32))


def draw_send_list(key, part):
    return routing(jax.random.fold_in(key, 5))[0]


def draw_pair_slots(key, part):
    return routing(jax.random.fold_in(key, 5))[1]


def draw_log_scales(key, part):
    long_axis = jax.random.uniform(jax.random.fold_in(key, 61), (BLOCKS, 1, G), jnp.float32, -1.0, -0.4)
    short_axes = jax.random.uniform(jax.random.fold_in(key, 62), (BLOCKS, 2, G), jnp.float32, -3.3, -2.7)
    return jnp.concatenate([long_axis, short_axes], axis=1)


def draw_cameras(key, part):
    keys = [jax.random.fold_in(key, 41 + step_at) for step_at in range(5)]
    quat = jax.random.uniform(keys[0], (N_VIEW, 4), jnp.float32, -1.0, 1.0)
    quat = quat + jnp.array([2.0, 0.0, 0.0, 0.0], jnp.float32)
    quat = quat / jnp.sqrt(jnp.sum(quat * quat, axis=1, keepdims=True))
    quat_w, quat_x, quat_y, quat_z = (quat[:, 0], quat[:, 1], quat[:, 2], quat[:, 3])
    rotation = jnp.stack([1.0 - 2.0 * (quat_y * quat_y + quat_z * quat_z), 2.0 * (quat_x * quat_y - quat_w * quat_z), 2.0 * (quat_x * quat_z + quat_w * quat_y), 2.0 * (quat_x * quat_y + quat_w * quat_z), 1.0 - 2.0 * (quat_x * quat_x + quat_z * quat_z), 2.0 * (quat_y * quat_z - quat_w * quat_x), 2.0 * (quat_x * quat_z - quat_w * quat_y), 2.0 * (quat_y * quat_z + quat_w * quat_x), 1.0 - 2.0 * (quat_x * quat_x + quat_y * quat_y)], axis=1)
    shift_side = jax.random.uniform(keys[1], (N_VIEW, 2), jnp.float32, -0.5, 0.5)
    shift_depth = jax.random.uniform(keys[2], (N_VIEW, 1), jnp.float32, 10.0, 12.0)
    image_width = TILE_COLS * 16.0
    image_height = TILES // TILE_COLS * 16.0
    focal = jax.random.uniform(keys[3], (N_VIEW, 1), jnp.float32, 0.9, 1.1) * image_width * 10.0 / 6.0
    centre = jax.random.uniform(keys[4], (N_VIEW, 2), jnp.float32, 0.95, 1.05) * jnp.array([image_width / 2.0, image_height / 2.0], jnp.float32)
    return jnp.concatenate([rotation, shift_side, shift_depth, focal, focal, centre], axis=1)


def shard_levels(key, extent, cuts, least, top_value):
    factor_of, own = 1.0, jax.random.fold_in(key, 6)
    for dim, blocks in cuts:
        steps = jnp.exp(jax.random.uniform(jax.random.fold_in(own, dim), (blocks,), jnp.float32, least / len(cuts), top_value / len(cuts)))
        factor_of = factor_of * jnp.repeat(steps, extent[dim] // blocks).reshape([-1 if axis == dim else 1 for axis in range(len(extent))])
    return factor_of


def scatter_about(stream_key, extent, width, most, shards=(), kind=jnp.bfloat16):
    result = jax.random.normal(stream_key, extent, jnp.float32) * width
    if len(shards) > 0:
        result = shard_levels(stream_key, extent, shards, -0.22, 0.18) * result
    return jnp.clip(result, min=-most, max=most).astype(kind)


def setup_inputs(seed: int = 0) -> dict:
    arg_keys = jax.random.split(jax.random.key(seed), 12)
    means = jnp.clip(jax.random.uniform(arg_keys[0], (BLOCKS, 3, G), jnp.float32, -3.0, 3.0) * shard_levels(arg_keys[0], (BLOCKS, 3, G), ((0, 32),), -0.4, 0.0), -3.0, 3.0)
    log_scales = draw_log_scales(jax.random.fold_in(arg_keys[11], 71), 0)
    rotations = scatter_about(arg_keys[2], (BLOCKS, 4, G), 1.0, 2.5, ((0, 32),), jnp.float32)
    opacity_logits = jnp.clip(jax.random.uniform(arg_keys[3], (BLOCKS, 1, G), jnp.float32, -3.0, 3.0) * shard_levels(arg_keys[3], (BLOCKS, 1, G), ((0, 32),), -0.4, 0.0), -3.0, 3.0)
    colour_coefs = scatter_about(arg_keys[4], (BLOCKS, 48, G), 0.25, 2.0, ((0, 32),), jnp.float32)
    cameras = draw_cameras(jax.random.fold_in(arg_keys[11], 71), 0)
    exposure = scatter_about(arg_keys[6], (N_VIEW, 12), 0.3, 1.0, ((0, 2),), jnp.float32)
    target = jnp.clip(1.0 * jax.random.uniform(arg_keys[7], (N_VIEW, TILES, 3, PIX), jnp.float32) ** shard_levels(arg_keys[7], (N_VIEW, TILES, 3, PIX), ((0, 2), (1, 16)), -0.2, 0.2), 0.0, 1.0)
    tile_ids = jax.vmap(lambda own: jax.random.permutation(own, TILES))(jax.random.split(arg_keys[8], N_VIEW)).reshape((N_VIEW, TILES)).astype(jnp.int32)
    send_list = draw_send_list(jax.random.fold_in(arg_keys[11], 71), 0)
    pair_slots = draw_pair_slots(jax.random.fold_in(arg_keys[11], 71), 0)
    return {"means": means, "log_scales": log_scales, "rotations": rotations, "opacity_logits": opacity_logits, "colour_coefs": colour_coefs, "cameras": cameras, "exposure": exposure, "target": target, "tile_ids": tile_ids, "send_list": send_list, "pair_slots": pair_slots}


SH_ZERO = 0.28209479177387814
SH_ONE = 0.4886025119029199
SH_TWO = (1.0925484305920792, -1.0925484305920792, 0.31539156525252005, -1.0925484305920792, 0.5462742152960396)
SH_THREE = (-0.5900435899266435, 2.890611442640554, -0.4570457994644658, 0.3731763325901154, -0.4570457994644658, 1.445305721320277, -0.5900435899266435)

def harmonics(dir_x, dir_y, dir_z):
    sq_x, sq_y, sq_z = (dir_x * dir_x, dir_y * dir_y, dir_z * dir_z)
    sh_basis = [SH_ZERO * jnp.ones_like(dir_x), -SH_ONE * dir_y, SH_ONE * dir_z, -SH_ONE * dir_x, SH_TWO[0] * dir_x * dir_y, SH_TWO[1] * dir_y * dir_z, SH_TWO[2] * (2.0 * sq_z - sq_x - sq_y), SH_TWO[3] * dir_x * dir_z, SH_TWO[4] * (sq_x - sq_y), SH_THREE[0] * dir_y * (3.0 * sq_x - sq_y), SH_THREE[1] * dir_x * dir_y * dir_z, SH_THREE[2] * dir_y * (4.0 * sq_z - sq_x - sq_y), SH_THREE[3] * dir_z * (2.0 * sq_z - 3.0 * sq_x - 3.0 * sq_y), SH_THREE[4] * dir_x * (4.0 * sq_z - sq_x - sq_y), SH_THREE[5] * dir_z * (sq_x - sq_y), SH_THREE[6] * dir_x * (sq_x - 3.0 * sq_y)]
    return jnp.stack(sh_basis, axis=1)

def project(pieces, camera):
    means, log_scales, rotations, opacity_logits, colour_coefs = pieces
    rotation = camera[0:9].reshape(3, 3)
    translation = camera[9:12]
    focal_x, focal_y, centre_x, centre_y = (camera[12], camera[13], camera[14], camera[15])
    position = [means[:, 0], means[:, 1], means[:, 2]]
    view_pos = [rotation[row_at, 0] * position[0] + rotation[row_at, 1] * position[1] + rotation[row_at, 2] * position[2] + translation[row_at] for row_at in range(3)]
    inv_depth = 1.0 / view_pos[2]
    quat_w = rotations[:, 0] + 3.0
    quat_x, quat_y, quat_z = (rotations[:, 1], rotations[:, 2], rotations[:, 3])
    quat_norm = jnp.sqrt(quat_w * quat_w + quat_x * quat_x + quat_y * quat_y + quat_z * quat_z)
    quat_w, quat_x, quat_y, quat_z = (quat_w / quat_norm, quat_x / quat_norm, quat_y / quat_norm, quat_z / quat_norm)
    spin_matrix = [[1.0 - 2.0 * (quat_y * quat_y + quat_z * quat_z), 2.0 * (quat_x * quat_y - quat_w * quat_z), 2.0 * (quat_x * quat_z + quat_w * quat_y)], [2.0 * (quat_x * quat_y + quat_w * quat_z), 1.0 - 2.0 * (quat_x * quat_x + quat_z * quat_z), 2.0 * (quat_y * quat_z - quat_w * quat_x)], [2.0 * (quat_x * quat_z - quat_w * quat_y), 2.0 * (quat_y * quat_z + quat_w * quat_x), 1.0 - 2.0 * (quat_x * quat_x + quat_y * quat_y)]]
    scales = jnp.exp(log_scales)
    world_frame = [[spin_matrix[row_at][col_at] * scales[:, col_at] for col_at in range(3)] for row_at in range(3)]
    jacobian = [[focal_x * inv_depth * rotation[0, col_at] - focal_x * view_pos[0] * inv_depth * inv_depth * rotation[2, col_at] for col_at in range(3)], [focal_y * inv_depth * rotation[1, col_at] - focal_y * view_pos[1] * inv_depth * inv_depth * rotation[2, col_at] for col_at in range(3)]]
    screen_frame = [[jacobian[row_at][0] * world_frame[0][col_at] + jacobian[row_at][1] * world_frame[1][col_at] + jacobian[row_at][2] * world_frame[2][col_at] for col_at in range(3)] for row_at in range(2)]
    sigma_xx = screen_frame[0][0] ** 2 + screen_frame[0][1] ** 2 + screen_frame[0][2] ** 2 + 0.3
    sigma_yy = screen_frame[1][0] ** 2 + screen_frame[1][1] ** 2 + screen_frame[1][2] ** 2 + 0.3
    sigma_xy = screen_frame[0][0] * screen_frame[1][0] + screen_frame[0][1] * screen_frame[1][1] + screen_frame[0][2] * screen_frame[1][2]
    determinant = sigma_xx * sigma_yy - sigma_xy * sigma_xy
    screen_x = focal_x * view_pos[0] * inv_depth + centre_x
    screen_y = focal_y * view_pos[1] * inv_depth + centre_y
    opacity = jax.nn.sigmoid(opacity_logits[:, 0])
    eye_pos = [-(rotation[0, col_at] * translation[0] + rotation[1, col_at] * translation[1] + rotation[2, col_at] * translation[2]) for col_at in range(3)]
    offsets = [position[col_at] - eye_pos[col_at] for col_at in range(3)]
    eye_dist = jnp.sqrt(offsets[0] ** 2 + offsets[1] ** 2 + offsets[2] ** 2)
    sh_basis = harmonics(offsets[0] / eye_dist, offsets[1] / eye_dist, offsets[2] / eye_dist)
    sh_coefs = colour_coefs.reshape(colour_coefs.shape[0], 16, 3, colour_coefs.shape[2])
    colour = jnp.maximum(0.5 + lax.optimization_barrier(jnp.sum(sh_basis[:, :, None, :] * sh_coefs, axis=1)), 0.0)
    shape_rows = jnp.stack([screen_x, screen_y, sigma_yy / determinant, -sigma_xy / determinant, sigma_xx / determinant, opacity], axis=1)
    return jnp.concatenate([shape_rows, colour], axis=1)

def composite(chosen_blk, live_mask, tile_id):
    pixel_index = jnp.arange(PIX, dtype=jnp.int32)
    pixel_x = (16 * (tile_id % TILE_COLS) + pixel_index % 16).astype(jnp.float32) + 0.5
    pixel_y = (16 * (tile_id // TILE_COLS) + pixel_index // 16).astype(jnp.float32) + 0.5
    gap_x = pixel_x[None, :, None] - chosen_blk[:, 0][:, None, :]
    gap_y = pixel_y[None, :, None] - chosen_blk[:, 1][:, None, :]
    falloff = 0.5 * (chosen_blk[:, 2][:, None, :] * gap_x * gap_x + chosen_blk[:, 4][:, None, :] * gap_y * gap_y) + chosen_blk[:, 3][:, None, :] * gap_x * gap_y
    alpha_vals = chosen_blk[:, 5][:, None, :] * jnp.exp(-falloff) * live_mask.astype(jnp.float32)[:, None, None]
    log_keep = jnp.log1p(-alpha_vals)
    slot_count, pixel_count, lane_count = log_keep.shape
    flat_keep = jnp.transpose(log_keep, (1, 0, 2)).reshape(pixel_count, slot_count * lane_count)
    before_sum = jnp.cumsum(flat_keep, axis=1) - flat_keep
    transmit = jnp.transpose(jnp.exp(before_sum).reshape(pixel_count, slot_count, lane_count), (1, 0, 2))
    return jnp.einsum('kpg,kcg->cp', alpha_vals * transmit, chosen_blk[:, 6:9], precision=lax.Precision.HIGHEST)

def reference(means, log_scales, rotations, opacity_logits, colour_coefs, cameras, exposure, target, tile_ids, send_list, pair_slots):
    renderer = jnp.arange(TILES, dtype=jnp.int32) // TILES_DEV
    safe_slot = jnp.maximum(pair_slots, 0)
    source = safe_slot // CAP
    place = safe_slot % CAP
    view_rows = jnp.arange(N_VIEW, dtype=jnp.int32)[:, None, None]
    local_ids = send_list[view_rows, source, renderer[None, :, None], place]
    block_ids = (local_ids // BLK_DEV * (N_SCENE * BLK_DEV) + source * BLK_DEV + local_ids % BLK_DEV).astype(jnp.int32)
    live_mask = pair_slots >= 0

    def forward(pieces, expo_all):

        def one_view(view_items):
            camera, expo, view_blocks, view_live, view_tiles = view_items
            projected = project(pieces, camera)

            def one_tile(tile_items):
                return composite(jnp.take(projected, tile_items[0], axis=0), tile_items[1], tile_items[2])
            shaded = lax.map(jax.checkpoint(one_tile), (view_blocks, view_live, view_tiles))
            mixing = jnp.eye(3, dtype=jnp.float32) + expo[0:9].reshape(3, 3)
            return jnp.einsum('ij,tjp->tip', mixing, shaded, precision=lax.Precision.HIGHEST) + expo[9:12][None, :, None]
        return lax.map(one_view, (cameras, expo_all, block_ids, live_mask, tile_ids))
    params = (means, log_scales, rotations, opacity_logits, colour_coefs)
    shown, backward = jax.vjp(forward, params, exposure)
    param_grads, grad_exposure = backward(shown - target)
    return (shown, param_grads[0], param_grads[1], param_grads[2], param_grads[3], param_grads[4], grad_exposure)
```

```python
import functools

import jax
import jax.numpy as jnp
from jax import lax
from jax.experimental import pallas as pl
from jax.experimental.pallas import tpu as pltpu
from jax.sharding import PartitionSpec as P

PIX = 256
TILE_COLS = 32


SH_ZERO = 0.28209479177387814
SH_ONE = 0.4886025119029199
SH_TWO = (
    1.0925484305920792,
    -1.0925484305920792,
    0.31539156525252005,
    -1.0925484305920792,
    0.5462742152960396,
)
SH_THREE = (
    -0.5900435899266435,
    2.890611442640554,
    -0.4570457994644658,
    0.3731763325901154,
    -0.4570457994644658,
    1.445305721320277,
    -0.5900435899266435,
)


def harmonics(dir_x, dir_y, dir_z):
    sq_x, sq_y, sq_z = (dir_x * dir_x, dir_y * dir_y, dir_z * dir_z)
    sh_basis = [
        SH_ZERO * jnp.ones_like(dir_x),
        -SH_ONE * dir_y,
        SH_ONE * dir_z,
        -SH_ONE * dir_x,
        SH_TWO[0] * dir_x * dir_y,
        SH_TWO[1] * dir_y * dir_z,
        SH_TWO[2] * (2.0 * sq_z - sq_x - sq_y),
        SH_TWO[3] * dir_x * dir_z,
        SH_TWO[4] * (sq_x - sq_y),
        SH_THREE[0] * dir_y * (3.0 * sq_x - sq_y),
        SH_THREE[1] * dir_x * dir_y * dir_z,
        SH_THREE[2] * dir_y * (4.0 * sq_z - sq_x - sq_y),
        SH_THREE[3] * dir_z * (2.0 * sq_z - 3.0 * sq_x - 3.0 * sq_y),
        SH_THREE[4] * dir_x * (4.0 * sq_z - sq_x - sq_y),
        SH_THREE[5] * dir_z * (sq_x - sq_y),
        SH_THREE[6] * dir_x * (sq_x - 3.0 * sq_y),
    ]
    return jnp.stack(sh_basis, axis=1)


def project(pieces, camera):
    means, log_scales, rotations, opacity_logits, colour_coefs = pieces
    rotation = camera[0:9].reshape(3, 3)
    translation = camera[9:12]
    focal_x, focal_y, centre_x, centre_y = (camera[12], camera[13], camera[14], camera[15])
    position = [means[:, 0], means[:, 1], means[:, 2]]
    view_pos = [
        rotation[row_at, 0] * position[0]
        + rotation[row_at, 1] * position[1]
        + rotation[row_at, 2] * position[2]
        + translation[row_at]
        for row_at in range(3)
    ]
    inv_depth = 1.0 / view_pos[2]
    quat_w = rotations[:, 0] + 3.0
    quat_x, quat_y, quat_z = (rotations[:, 1], rotations[:, 2], rotations[:, 3])
    quat_norm = jnp.sqrt(quat_w * quat_w + quat_x * quat_x + quat_y * quat_y + quat_z * quat_z)
    quat_w, quat_x, quat_y, quat_z = (
        quat_w / quat_norm,
        quat_x / quat_norm,
        quat_y / quat_norm,
        quat_z / quat_norm,
    )
    spin_matrix = [
        [
            1.0 - 2.0 * (quat_y * quat_y + quat_z * quat_z),
            2.0 * (quat_x * quat_y - quat_w * quat_z),
            2.0 * (quat_x * quat_z + quat_w * quat_y),
        ],
        [
            2.0 * (quat_x * quat_y + quat_w * quat_z),
            1.0 - 2.0 * (quat_x * quat_x + quat_z * quat_z),
            2.0 * (quat_y * quat_z - quat_w * quat_x),
        ],
        [
            2.0 * (quat_x * quat_z - quat_w * quat_y),
            2.0 * (quat_y * quat_z + quat_w * quat_x),
            1.0 - 2.0 * (quat_x * quat_x + quat_y * quat_y),
        ],
    ]
    scales = jnp.exp(log_scales)
    world_frame = [
        [spin_matrix[row_at][col_at] * scales[:, col_at] for col_at in range(3)]
        for row_at in range(3)
    ]
    jacobian = [
        [
            focal_x * inv_depth * rotation[0, col_at]
            - focal_x * view_pos[0] * inv_depth * inv_depth * rotation[2, col_at]
            for col_at in range(3)
        ],
        [
            focal_y * inv_depth * rotation[1, col_at]
            - focal_y * view_pos[1] * inv_depth * inv_depth * rotation[2, col_at]
            for col_at in range(3)
        ],
    ]
    screen_frame = [
        [
            jacobian[row_at][0] * world_frame[0][col_at]
            + jacobian[row_at][1] * world_frame[1][col_at]
            + jacobian[row_at][2] * world_frame[2][col_at]
            for col_at in range(3)
        ]
        for row_at in range(2)
    ]
    sigma_xx = screen_frame[0][0] ** 2 + screen_frame[0][1] ** 2 + screen_frame[0][2] ** 2 + 0.3
    sigma_yy = screen_frame[1][0] ** 2 + screen_frame[1][1] ** 2 + screen_frame[1][2] ** 2 + 0.3
    sigma_xy = (
        screen_frame[0][0] * screen_frame[1][0]
        + screen_frame[0][1] * screen_frame[1][1]
        + screen_frame[0][2] * screen_frame[1][2]
    )
    determinant = sigma_xx * sigma_yy - sigma_xy * sigma_xy
    screen_x = focal_x * view_pos[0] * inv_depth + centre_x
    screen_y = focal_y * view_pos[1] * inv_depth + centre_y
    opacity = jax.nn.sigmoid(opacity_logits[:, 0])
    eye_pos = [
        -(
            rotation[0, col_at] * translation[0]
            + rotation[1, col_at] * translation[1]
            + rotation[2, col_at] * translation[2]
        )
        for col_at in range(3)
    ]
    offsets = [position[col_at] - eye_pos[col_at] for col_at in range(3)]
    eye_dist = jnp.sqrt(offsets[0] ** 2 + offsets[1] ** 2 + offsets[2] ** 2)
    sh_basis = harmonics(offsets[0] / eye_dist, offsets[1] / eye_dist, offsets[2] / eye_dist)
    sh_coefs = colour_coefs.reshape(colour_coefs.shape[0], 16, 3, colour_coefs.shape[2])
    colour = jnp.maximum(0.5 + jnp.sum(sh_basis[:, :, None, :] * sh_coefs, axis=1), 0.0)
    shape_rows = jnp.stack(
        [
            screen_x,
            screen_y,
            sigma_yy / determinant,
            -sigma_xy / determinant,
            sigma_xx / determinant,
            opacity,
        ],
        axis=1,
    )
    return jnp.concatenate([shape_rows, colour], axis=1)


LOG2E = 1.4426950408889634
FEATURES = 9


def split_pair(values):
    high = values.astype(jnp.bfloat16)
    low = (values - high.astype(jnp.float32)).astype(jnp.bfloat16)
    return jnp.concatenate([high, low], axis=1)


def render_kernel(
    tile_ids,
    slots,
    exposure,
    incoming,
    target,
    shown,
    grads,
    weight,
    ratio,
    weight_pair,
    expo_sum,
    before_mat,
    after_mat,
    powers,
):
    tile_count, slot_count = slots.shape
    lanes = incoming.shape[2]
    row_at = lax.broadcasted_iota(jnp.int32, (2 * lanes, 2 * lanes), 0) % lanes
    col_at = lax.broadcasted_iota(jnp.int32, (2 * lanes, 2 * lanes), 1)
    total = col_at >= lanes
    before_mat[...] = jnp.where(total | (row_at < col_at), 1.0, 0.0).astype(jnp.bfloat16)
    after_mat[...] = jnp.where(total | (row_at > col_at), 1.0, 0.0).astype(jnp.bfloat16)
    power_at = lax.broadcasted_iota(jnp.int32, (8, PIX), 0)
    pixel_at = lax.broadcasted_iota(jnp.int32, (8, PIX), 1)
    side_x = (pixel_at % 16).astype(jnp.float32) - 7.5
    side_y = (pixel_at // 16).astype(jnp.float32) - 7.5
    picks = [jnp.ones_like(side_x), side_x, side_y, side_x * side_x, side_x * side_y, side_y * side_y]
    table = jnp.zeros((8, PIX), jnp.float32)
    for at, pick in enumerate(picks):
        table = jnp.where(power_at == at, pick, table)
    powers[...] = table.astype(jnp.bfloat16)
    grads[...] = jnp.zeros_like(grads)
    expo_sum[...] = jnp.zeros_like(expo_sum)
    mixing = [
        [exposure[0, 3 * i + j] + (1.0 if i == j else 0.0) for j in range(3)] for i in range(3)
    ]
    offset = [exposure[0, 9 + i] for i in range(3)]
    local_x = [
        lax.broadcasted_iota(jnp.int32, (8, lanes), 0).astype(jnp.float32) + (8.0 * half - 7.5)
        for half in range(2)
    ]
    zero_rows = jnp.zeros((2, lanes), jnp.float32)

    def load(tile, at, centre_x, centre_y):
        block = incoming[slots[tile, at]]
        rows = [block[i : i + 1] for i in range(FEATURES)]
        rows[0] = rows[0] - centre_x
        rows[1] = rows[1] - centre_y
        return rows, block[6:9]

    def one_tile(tile, live):
        tile_id = tile_ids[0, tile]
        centre_x = (16 * (tile_id % TILE_COLS) + 8).astype(jnp.float32)
        centre_y = (16 * (tile_id // TILE_COLS) + 8).astype(jnp.float32)
        carry = None
        shade = None
        for at in range(live):
            rows, colour = load(tile, at, centre_x, centre_y)
            wide = [jnp.broadcast_to(row, (8, lanes)) for row in rows[:6]]
            gap_x = [side - wide[0] for side in local_x]
            scaled_a = wide[2] * (-0.5 * LOG2E)
            scaled_b = wide[3] * (-LOG2E)
            scaled_c = wide[4] * (-0.5 * LOG2E)
            part_x = [scaled_a * gap * gap for gap in gap_x]
            pieces = []
            for line in range(PIX // 16):
                gap_y = (line - 7.5) - wide[1]
                part_y = scaled_c * gap_y * gap_y
                slope = scaled_b * gap_y
                for half in range(2):
                    pieces.append(
                        wide[5] * jnp.exp2(part_x[half] + gap_x[half] * slope + part_y)
                    )
            alpha = jnp.concatenate(pieces, axis=0)
            log_keep = jnp.log(1.0 - alpha)
            sums = jnp.dot(
                split_pair(log_keep), before_mat[...], preferred_element_type=jnp.float32
            )
            inside = sums[:, :lanes]
            if at > 0:
                inside = inside + carry
            if at + 1 < live:
                carry = sums[:, lanes:] if at == 0 else carry + sums[:, lanes:]
            seen = alpha * jnp.exp(inside)
            pair = split_pair(seen)
            weight[at] = seen
            ratio[at] = alpha * jnp.exp(-log_keep)
            weight_pair[at] = pair
            high = colour.astype(jnp.bfloat16).astype(jnp.float32)
            low = colour - high
            left = jnp.concatenate([high, low, zero_rows], axis=0)
            right = jnp.concatenate([high, jnp.zeros((5, lanes), jnp.float32)], axis=0)
            mixed = jnp.concatenate([left, right], axis=1).astype(jnp.bfloat16)
            term = lax.dot_general(
                mixed, pair, (((1,), (1,)), ((), ())), preferred_element_type=jnp.float32
            )
            shade = term if at == 0 else shade + term
        goal = target[0, tile]
        tone = [shade[i : i + 1] + shade[i + 3 : i + 4] for i in range(3)]
        image = [
            mixing[i][0] * tone[0] + mixing[i][1] * tone[1] + mixing[i][2] * tone[2] + offset[i]
            for i in range(3)
        ]
        shown[0, tile] = jnp.concatenate(image, axis=0)
        miss = [image[i] - goal[i : i + 1] for i in range(3)]
        expo_sum[...] += jnp.concatenate(
            [miss[i] * tone[j] for i in range(3) for j in range(3)] + miss, axis=0
        )
        back = jnp.concatenate(
            [
                mixing[0][j] * miss[0] + mixing[1][j] * miss[1] + mixing[2][j] * miss[2]
                for j in range(3)
            ],
            axis=0,
        )
        back_high = back.astype(jnp.bfloat16).astype(jnp.float32)
        back_low = back - back_high
        back_left = jnp.concatenate(
            [back_high, back_low, jnp.zeros((2, PIX), jnp.float32)], axis=0
        ).astype(jnp.bfloat16)
        back_side = jnp.transpose(
            jnp.concatenate(
                [back_high, back_high, back_low, jnp.zeros((7, PIX), jnp.float32)], axis=0
            )
        ).astype(jnp.bfloat16)
        carry = None
        for at in reversed(range(live)):
            rows, colour = load(tile, at, centre_x, centre_y)
            high = colour.astype(jnp.bfloat16).astype(jnp.float32)
            low = colour - high
            colour_side = jnp.concatenate(
                [high, low, high, jnp.zeros((7, lanes), jnp.float32)], axis=0
            ).astype(jnp.bfloat16)
            pull = jnp.dot(back_side, colour_side, preferred_element_type=jnp.float32)
            gain = weight[at] * pull
            sums = jnp.dot(split_pair(gain), after_mat[...], preferred_element_type=jnp.float32)
            behind = sums[:, :lanes]
            if at + 1 < live:
                behind = behind + carry
            if at > 0:
                carry = sums[:, lanes:] if at + 1 == live else carry + sums[:, lanes:]
            heat = gain - behind * ratio[at]
            moments = jnp.dot(powers[...], split_pair(heat), preferred_element_type=jnp.float32)
            moments = moments[:, :lanes] + moments[:, lanes:]
            tint = jnp.dot(back_left, weight_pair[at], preferred_element_type=jnp.float32)
            tint = tint[:, :lanes] + tint[:, lanes:]
            tint = tint[0:3] + tint[3:6]
            pos_x, pos_y, con_a, con_b, con_c, opacity = rows[:6]
            m_one, m_x, m_y, m_xx, m_xy, m_yy = [moments[i : i + 1] for i in range(6)]
            d_x = m_x - pos_x * m_one
            d_y = m_y - pos_y * m_one
            d_xx = m_xx - pos_x * (m_x + d_x)
            d_xy = m_xy - pos_x * m_y - pos_y * d_x
            d_yy = m_yy - pos_y * (m_y + d_y)
            grads[slots[tile, at], 0:FEATURES] += jnp.concatenate(
                [
                    con_a * d_x + con_b * d_y,
                    con_b * d_x + con_c * d_y,
                    -0.5 * d_xx,
                    -d_xy,
                    -0.5 * d_yy,
                    m_one / opacity,
                    tint,
                ],
                axis=0,
            )

    def tile_step(tile, unused):
        live = jnp.int32(0)
        for at in range(slot_count):
            live = live + jnp.where(slots[tile, at] >= 0, 1, 0)
        for number in range(1, slot_count + 1):
            pl.when(live == number)(functools.partial(one_tile, tile, number))
        return unused

    lax.fori_loop(0, tile_count, tile_step, 0)
    sums = jnp.sum(expo_sum[...], axis=1, keepdims=True)
    lane_at = lax.broadcasted_iota(jnp.int32, (12, lanes), 1)
    row_at = lax.broadcasted_iota(jnp.int32, (12, lanes), 0)
    spread = jnp.sum(jnp.where(lane_at == row_at, sums, 0.0), axis=0, keepdims=True)
    grads[:, FEATURES : FEATURES + 1] = jnp.broadcast_to(spread[None], (grads.shape[0], 1, lanes))


def render(tile_ids, slots, exposure, incoming, target):
    slot_count = slots.shape[1]
    lanes = incoming.shape[2]
    smem = pl.BlockSpec(memory_space=pltpu.SMEM)
    vmem = pl.BlockSpec(memory_space=pltpu.VMEM)
    return pl.pallas_call(
        render_kernel,
        out_shape=(
            jax.ShapeDtypeStruct(target.shape, jnp.float32),
            jax.ShapeDtypeStruct((incoming.shape[0], FEATURES + 1, lanes), jnp.float32),
        ),
        in_specs=[smem, smem, smem, vmem, vmem],
        out_specs=(vmem, vmem),
        scratch_shapes=[
            pltpu.VMEM((slot_count, PIX, lanes), jnp.float32),
            pltpu.VMEM((slot_count, PIX, lanes), jnp.float32),
            pltpu.VMEM((slot_count, PIX, 2 * lanes), jnp.bfloat16),
            pltpu.VMEM((12, PIX), jnp.float32),
            pltpu.VMEM((2 * lanes, 2 * lanes), jnp.bfloat16),
            pltpu.VMEM((2 * lanes, 2 * lanes), jnp.bfloat16),
            pltpu.VMEM((8, PIX), jnp.bfloat16),
        ],
        compiler_params=pltpu.CompilerParams(vmem_limit_bytes=32 * 1024 * 1024),
    )(tile_ids, slots, exposure, incoming, target)


def local(
    means,
    log_scales,
    rotations,
    opacity_logits,
    colour_coefs,
    cameras,
    exposure,
    target,
    tile_ids,
    send_list,
    pair_slots,
):
    view_count = lax.axis_size("view")
    scene_count = lax.axis_size("scene")
    own_params = (means, log_scales, rotations, opacity_logits, colour_coefs)
    per_device = means.shape[0]
    owned_count = per_device * view_count
    feature_count = 9
    lane_count = means.shape[2]
    capacity = send_list.shape[3]
    own_proj, unproject = jax.vjp(
        lambda *pieces: jax.vmap(lambda cam_row: project(pieces, cam_row))(cameras), *own_params
    )
    arrived = lax.all_to_all(own_proj, "view", split_axis=0, concat_axis=0, tiled=True)
    projected = arrived.reshape(owned_count, feature_count, lane_count)
    send_picks = send_list[0, 0]
    outgoing = jnp.take(projected, jnp.maximum(send_picks, 0).reshape(-1), axis=0)
    outgoing = (
        outgoing.reshape(scene_count, capacity, feature_count, lane_count)
        * (send_picks >= 0).astype(jnp.float32)[:, :, None, None]
    )
    incoming = lax.all_to_all(outgoing, "scene", split_axis=0, concat_axis=0, tiled=True).reshape(
        scene_count * capacity, feature_count, lane_count
    )
    shown_tiles, grad_incoming = render(tile_ids, pair_slots[0], exposure, incoming, target)
    returned = lax.all_to_all(
        grad_incoming.reshape(scene_count, capacity, feature_count + 1, lane_count),
        "scene",
        split_axis=0,
        concat_axis=0,
        tiled=True,
    )
    exposure_grad = jnp.sum(returned[:, 0, feature_count, 0:12], axis=0)
    returned = returned[:, :, 0:feature_count]
    home_index = jnp.where(send_picks >= 0, send_picks, owned_count).reshape(-1)
    grad_projected = (
        jnp.zeros((owned_count, feature_count, lane_count), jnp.float32)
        .at[home_index]
        .add(returned.reshape(-1, feature_count, lane_count), mode="drop")
    )
    sent_back = lax.all_to_all(
        grad_projected.reshape(view_count, per_device, feature_count, lane_count),
        "view",
        split_axis=0,
        concat_axis=0,
        tiled=True,
    )
    param_grads = unproject(sent_back)
    return (
        shown_tiles,
        param_grads[0],
        param_grads[1],
        param_grads[2],
        param_grads[3],
        param_grads[4],
        exposure_grad[None],
    )


def solution(mesh):
    return jax.shard_map(
        local,
        mesh=mesh,
        in_specs=(
            P(("view", "scene"), None, None),
            P(("view", "scene"), None, None),
            P(("view", "scene"), None, None),
            P(("view", "scene"), None, None),
            P(("view", "scene"), None, None),
            P(),
            P("view", None),
            P("view", "scene", None, None),
            P("view", "scene"),
            P("view", "scene", None, None),
            P("view", "scene", None),
        ),
        out_specs=(
            P("view", "scene", None, None),
            P(("view", "scene"), None, None),
            P(("view", "scene"), None, None),
            P(("view", "scene"), None, None),
            P(("view", "scene"), None, None),
            P(("view", "scene"), None, None),
            P("view", None),
        ),
        check_vma=False,
    )
```

```python
import functools

import jax
import jax.numpy as jnp
from jax import lax
from jax.experimental import pallas as pl
from jax.experimental.pallas import tpu as pltpu
from jax.sharding import PartitionSpec as P

PIX = 256
TILE_COLS = 32

FEATURES = 9

SH_ZERO = 0.28209479177387814
SH_ONE = 0.4886025119029199
SH_TWO = (
    1.0925484305920792,
    -1.0925484305920792,
    0.31539156525252005,
    -1.0925484305920792,
    0.5462742152960396,
)
SH_THREE = (
    -0.5900435899266435,
    2.890611442640554,
    -0.4570457994644658,
    0.3731763325901154,
    -0.4570457994644658,
    1.445305721320277,
    -0.5900435899266435,
)


def harmonics(dir_x, dir_y, dir_z):
    sq_x, sq_y, sq_z = (dir_x * dir_x, dir_y * dir_y, dir_z * dir_z)
    sh_basis = [
        SH_ZERO * jnp.ones_like(dir_x),
        -SH_ONE * dir_y,
        SH_ONE * dir_z,
        -SH_ONE * dir_x,
        SH_TWO[0] * dir_x * dir_y,
        SH_TWO[1] * dir_y * dir_z,
        SH_TWO[2] * (2.0 * sq_z - sq_x - sq_y),
        SH_TWO[3] * dir_x * dir_z,
        SH_TWO[4] * (sq_x - sq_y),
        SH_THREE[0] * dir_y * (3.0 * sq_x - sq_y),
        SH_THREE[1] * dir_x * dir_y * dir_z,
        SH_THREE[2] * dir_y * (4.0 * sq_z - sq_x - sq_y),
        SH_THREE[3] * dir_z * (2.0 * sq_z - 3.0 * sq_x - 3.0 * sq_y),
        SH_THREE[4] * dir_x * (4.0 * sq_z - sq_x - sq_y),
        SH_THREE[5] * dir_z * (sq_x - sq_y),
        SH_THREE[6] * dir_x * (sq_x - 3.0 * sq_y),
    ]
    return sh_basis


def project(camera, position, log_scales, rotations, opacity_logits, colour_coefs):
    rotation = [camera[0:3], camera[3:6], camera[6:9]]
    translation = camera[9:12]
    focal_x, focal_y, centre_x, centre_y = camera[12:16]
    view_pos = [
        rotation[row_at][0] * position[0]
        + rotation[row_at][1] * position[1]
        + rotation[row_at][2] * position[2]
        + translation[row_at]
        for row_at in range(3)
    ]
    inv_depth = 1.0 / view_pos[2]
    quat_w = rotations[0] + 3.0
    quat_x, quat_y, quat_z = (rotations[1], rotations[2], rotations[3])
    quat_norm = jnp.sqrt(quat_w * quat_w + quat_x * quat_x + quat_y * quat_y + quat_z * quat_z)
    quat_w, quat_x, quat_y, quat_z = (
        quat_w / quat_norm,
        quat_x / quat_norm,
        quat_y / quat_norm,
        quat_z / quat_norm,
    )
    spin_matrix = [
        [
            1.0 - 2.0 * (quat_y * quat_y + quat_z * quat_z),
            2.0 * (quat_x * quat_y - quat_w * quat_z),
            2.0 * (quat_x * quat_z + quat_w * quat_y),
        ],
        [
            2.0 * (quat_x * quat_y + quat_w * quat_z),
            1.0 - 2.0 * (quat_x * quat_x + quat_z * quat_z),
            2.0 * (quat_y * quat_z - quat_w * quat_x),
        ],
        [
            2.0 * (quat_x * quat_z - quat_w * quat_y),
            2.0 * (quat_y * quat_z + quat_w * quat_x),
            1.0 - 2.0 * (quat_x * quat_x + quat_y * quat_y),
        ],
    ]
    scales = [jnp.exp(row) for row in log_scales]
    world_frame = [
        [spin_matrix[row_at][col_at] * scales[col_at] for col_at in range(3)]
        for row_at in range(3)
    ]
    jacobian = [
        [
            focal_x * inv_depth * rotation[0][col_at]
            - focal_x * view_pos[0] * inv_depth * inv_depth * rotation[2][col_at]
            for col_at in range(3)
        ],
        [
            focal_y * inv_depth * rotation[1][col_at]
            - focal_y * view_pos[1] * inv_depth * inv_depth * rotation[2][col_at]
            for col_at in range(3)
        ],
    ]
    screen_frame = [
        [
            jacobian[row_at][0] * world_frame[0][col_at]
            + jacobian[row_at][1] * world_frame[1][col_at]
            + jacobian[row_at][2] * world_frame[2][col_at]
            for col_at in range(3)
        ]
        for row_at in range(2)
    ]
    sigma_xx = screen_frame[0][0] ** 2 + screen_frame[0][1] ** 2 + screen_frame[0][2] ** 2 + 0.3
    sigma_yy = screen_frame[1][0] ** 2 + screen_frame[1][1] ** 2 + screen_frame[1][2] ** 2 + 0.3
    sigma_xy = (
        screen_frame[0][0] * screen_frame[1][0]
        + screen_frame[0][1] * screen_frame[1][1]
        + screen_frame[0][2] * screen_frame[1][2]
    )
    determinant = sigma_xx * sigma_yy - sigma_xy * sigma_xy
    screen_x = focal_x * view_pos[0] * inv_depth + centre_x
    screen_y = focal_y * view_pos[1] * inv_depth + centre_y
    opacity = jax.nn.sigmoid(opacity_logits)
    eye_pos = [
        -(
            rotation[0][col_at] * translation[0]
            + rotation[1][col_at] * translation[1]
            + rotation[2][col_at] * translation[2]
        )
        for col_at in range(3)
    ]
    offsets = [position[col_at] - eye_pos[col_at] for col_at in range(3)]
    eye_dist = jnp.sqrt(offsets[0] ** 2 + offsets[1] ** 2 + offsets[2] ** 2)
    sh_basis = harmonics(offsets[0] / eye_dist, offsets[1] / eye_dist, offsets[2] / eye_dist)
    colour = []
    for channel in range(3):
        total = sh_basis[0] * colour_coefs[channel]
        for order in range(1, 16):
            total = total + sh_basis[order] * colour_coefs[3 * order + channel]
        colour.append(jnp.maximum(0.5 + total, 0.0))
    return [
        screen_x,
        screen_y,
        sigma_yy / determinant,
        -sigma_xy / determinant,
        sigma_xx / determinant,
        opacity,
    ] + colour


LOG2E = 1.4426950408889634


def split_pair(values):
    high = values.astype(jnp.bfloat16)
    low = (values - high.astype(jnp.float32)).astype(jnp.bfloat16)
    return jnp.concatenate([high, low], axis=1)


def render_kernel(
    tile_ids,
    slots,
    exposure,
    incoming,
    target,
    shown,
    grads,
    weight,
    ratio,
    weight_pair,
    expo_sum,
    before_mat,
    after_mat,
    powers,
):
    tile_count, slot_count = slots.shape
    lanes = incoming.shape[2]
    row_at = lax.broadcasted_iota(jnp.int32, (2 * lanes, 2 * lanes), 0) % lanes
    col_at = lax.broadcasted_iota(jnp.int32, (2 * lanes, 2 * lanes), 1)
    total = col_at >= lanes
    before_mat[...] = jnp.where(total | (row_at < col_at), 1.0, 0.0).astype(jnp.bfloat16)
    after_mat[...] = jnp.where(total | (row_at > col_at), 1.0, 0.0).astype(jnp.bfloat16)
    power_at = lax.broadcasted_iota(jnp.int32, (8, PIX), 0)
    pixel_at = lax.broadcasted_iota(jnp.int32, (8, PIX), 1)
    side_x = (pixel_at % 16).astype(jnp.float32) - 7.5
    side_y = (pixel_at // 16).astype(jnp.float32) - 7.5
    picks = [jnp.ones_like(side_x), side_x, side_y, side_x * side_x, side_x * side_y, side_y * side_y]
    table = jnp.zeros((8, PIX), jnp.float32)
    for at, pick in enumerate(picks):
        table = jnp.where(power_at == at, pick, table)
    powers[...] = table.astype(jnp.bfloat16)
    grads[...] = jnp.zeros_like(grads)
    expo_sum[...] = jnp.zeros_like(expo_sum)
    mixing = [
        [exposure[0, 3 * i + j] + (1.0 if i == j else 0.0) for j in range(3)] for i in range(3)
    ]
    offset = [exposure[0, 9 + i] for i in range(3)]
    local_x = [
        lax.broadcasted_iota(jnp.int32, (8, lanes), 0).astype(jnp.float32) + (8.0 * half - 7.5)
        for half in range(2)
    ]
    zero_rows = jnp.zeros((2, lanes), jnp.float32)

    def load(tile, at, centre_x, centre_y):
        block = incoming[slots[tile, at]]
        rows = [block[i : i + 1] for i in range(FEATURES)]
        rows[0] = rows[0] - centre_x
        rows[1] = rows[1] - centre_y
        return rows, block[6:9]

    def one_tile(tile, live):
        tile_id = tile_ids[0, tile]
        centre_x = (16 * (tile_id % TILE_COLS) + 8).astype(jnp.float32)
        centre_y = (16 * (tile_id // TILE_COLS) + 8).astype(jnp.float32)
        carry = None
        shade = None
        for at in range(live):
            rows, colour = load(tile, at, centre_x, centre_y)
            wide = [jnp.broadcast_to(row, (8, lanes)) for row in rows[:6]]
            gap_x = [side - wide[0] for side in local_x]
            scaled_a = wide[2] * (-0.5 * LOG2E)
            scaled_b = wide[3] * (-LOG2E)
            scaled_c = wide[4] * (-0.5 * LOG2E)
            part_x = [scaled_a * gap * gap for gap in gap_x]
            pieces = []
            for line in range(PIX // 16):
                gap_y = (line - 7.5) - wide[1]
                part_y = scaled_c * gap_y * gap_y
                slope = scaled_b * gap_y
                for half in range(2):
                    pieces.append(
                        wide[5] * jnp.exp2(part_x[half] + gap_x[half] * slope + part_y)
                    )
            alpha = jnp.concatenate(pieces, axis=0)
            log_keep = jnp.log(1.0 - alpha)
            sums = jnp.dot(
                split_pair(log_keep), before_mat[...], preferred_element_type=jnp.float32
            )
            inside = sums[:, :lanes]
            if at > 0:
                inside = inside + carry
            if at + 1 < live:
                carry = sums[:, lanes:] if at == 0 else carry + sums[:, lanes:]
            seen = alpha * jnp.exp(inside)
            pair = split_pair(seen)
            weight[at] = seen
            ratio[at] = alpha * jnp.exp(-log_keep)
            weight_pair[at] = pair
            high = colour.astype(jnp.bfloat16).astype(jnp.float32)
            low = colour - high
            left = jnp.concatenate([high, low, zero_rows], axis=0)
            right = jnp.concatenate([high, jnp.zeros((5, lanes), jnp.float32)], axis=0)
            mixed = jnp.concatenate([left, right], axis=1).astype(jnp.bfloat16)
            term = lax.dot_general(
                mixed, pair, (((1,), (1,)), ((), ())), preferred_element_type=jnp.float32
            )
            shade = term if at == 0 else shade + term
        goal = target[0, tile]
        tone = [shade[i : i + 1] + shade[i + 3 : i + 4] for i in range(3)]
        image = [
            mixing[i][0] * tone[0] + mixing[i][1] * tone[1] + mixing[i][2] * tone[2] + offset[i]
            for i in range(3)
        ]
        shown[0, tile] = jnp.concatenate(image, axis=0)
        miss = [image[i] - goal[i : i + 1] for i in range(3)]
        expo_sum[...] += jnp.concatenate(
            [miss[i] * tone[j] for i in range(3) for j in range(3)] + miss, axis=0
        )
        back = jnp.concatenate(
            [
                mixing[0][j] * miss[0] + mixing[1][j] * miss[1] + mixing[2][j] * miss[2]
                for j in range(3)
            ],
            axis=0,
        )
        back_high = back.astype(jnp.bfloat16).astype(jnp.float32)
        back_low = back - back_high
        back_left = jnp.concatenate(
            [back_high, back_low, jnp.zeros((2, PIX), jnp.float32)], axis=0
        ).astype(jnp.bfloat16)
        back_side = jnp.transpose(
            jnp.concatenate(
                [back_high, back_high, back_low, jnp.zeros((7, PIX), jnp.float32)], axis=0
            )
        ).astype(jnp.bfloat16)
        carry = None
        for at in reversed(range(live)):
            rows, colour = load(tile, at, centre_x, centre_y)
            high = colour.astype(jnp.bfloat16).astype(jnp.float32)
            low = colour - high
            colour_side = jnp.concatenate(
                [high, low, high, jnp.zeros((7, lanes), jnp.float32)], axis=0
            ).astype(jnp.bfloat16)
            pull = jnp.dot(back_side, colour_side, preferred_element_type=jnp.float32)
            gain = weight[at] * pull
            sums = jnp.dot(split_pair(gain), after_mat[...], preferred_element_type=jnp.float32)
            behind = sums[:, :lanes]
            if at + 1 < live:
                behind = behind + carry
            if at > 0:
                carry = sums[:, lanes:] if at + 1 == live else carry + sums[:, lanes:]
            heat = gain - behind * ratio[at]
            moments = jnp.dot(powers[...], split_pair(heat), preferred_element_type=jnp.float32)
            moments = moments[:, :lanes] + moments[:, lanes:]
            tint = jnp.dot(back_left, weight_pair[at], preferred_element_type=jnp.float32)
            tint = tint[:, :lanes] + tint[:, lanes:]
            tint = tint[0:3] + tint[3:6]
            pos_x, pos_y, con_a, con_b, con_c, opacity = rows[:6]
            m_one, m_x, m_y, m_xx, m_xy, m_yy = [moments[i : i + 1] for i in range(6)]
            d_x = m_x - pos_x * m_one
            d_y = m_y - pos_y * m_one
            d_xx = m_xx - pos_x * (m_x + d_x)
            d_xy = m_xy - pos_x * m_y - pos_y * d_x
            d_yy = m_yy - pos_y * (m_y + d_y)
            grads[slots[tile, at], 0:FEATURES] += jnp.concatenate(
                [
                    con_a * d_x + con_b * d_y,
                    con_b * d_x + con_c * d_y,
                    -0.5 * d_xx,
                    -d_xy,
                    -0.5 * d_yy,
                    m_one / opacity,
                    tint,
                ],
                axis=0,
            )

    def tile_step(tile, unused):
        live = jnp.int32(0)
        for at in range(slot_count):
            live = live + jnp.where(slots[tile, at] >= 0, 1, 0)
        for number in range(1, slot_count + 1):
            pl.when(live == number)(functools.partial(one_tile, tile, number))
        return unused

    lax.fori_loop(0, tile_count, tile_step, 0)
    sums = jnp.sum(expo_sum[...], axis=1, keepdims=True)
    lane_at = lax.broadcasted_iota(jnp.int32, (12, lanes), 1)
    row_at = lax.broadcasted_iota(jnp.int32, (12, lanes), 0)
    spread = jnp.sum(jnp.where(lane_at == row_at, sums, 0.0), axis=0, keepdims=True)
    grads[:, FEATURES : FEATURES + 1] = jnp.broadcast_to(spread[None], (grads.shape[0], 1, lanes))


def render(tile_ids, slots, exposure, incoming, target):
    slot_count = slots.shape[1]
    lanes = incoming.shape[2]
    smem = pl.BlockSpec(memory_space=pltpu.SMEM)
    vmem = pl.BlockSpec(memory_space=pltpu.VMEM)
    return pl.pallas_call(
        render_kernel,
        out_shape=(
            jax.ShapeDtypeStruct(target.shape, jnp.float32),
            jax.ShapeDtypeStruct((incoming.shape[0], FEATURES + 1, lanes), jnp.float32),
        ),
        in_specs=[smem, smem, smem, vmem, vmem],
        out_specs=(vmem, vmem),
        scratch_shapes=[
            pltpu.VMEM((slot_count, PIX, lanes), jnp.float32),
            pltpu.VMEM((slot_count, PIX, lanes), jnp.float32),
            pltpu.VMEM((slot_count, PIX, 2 * lanes), jnp.bfloat16),
            pltpu.VMEM((12, PIX), jnp.float32),
            pltpu.VMEM((2 * lanes, 2 * lanes), jnp.bfloat16),
            pltpu.VMEM((2 * lanes, 2 * lanes), jnp.bfloat16),
            pltpu.VMEM((8, PIX), jnp.bfloat16),
        ],
        compiler_params=pltpu.CompilerParams(vmem_limit_bytes=32 * 1024 * 1024),
        name="render",
    )(tile_ids, slots, exposure, incoming, target)


def padded(rows):
    return (rows + 7) // 8 * 8


def camera_rows(cameras, block_count):
    view_count = cameras.shape[0]
    shape = (view_count * block_count, 128)
    view_at = lax.broadcasted_iota(jnp.int32, shape, 0) // block_count
    entries = []
    for entry in range(16):
        value = jnp.full(shape, cameras[0, entry])
        for view in range(1, view_count):
            value = jnp.where(view_at == view, cameras[view, entry], value)
        entries.append(value)
    return entries


def parameter_rows(refs, view_count):
    block_count = refs[0].shape[0]

    def row(ref, at):
        own = [ref[block, at : at + 1] for block in range(block_count)]
        return jnp.concatenate(own * view_count, axis=0)

    means, log_scales, rotations, opacity_logits, colour_coefs = refs
    return (
        [row(means, at) for at in range(3)],
        [row(log_scales, at) for at in range(3)],
        [row(rotations, at) for at in range(4)],
        row(opacity_logits, 0),
        [row(colour_coefs, at) for at in range(48)],
    )


def fill(rows, count, lanes):
    return rows if count == 0 else rows + [jnp.zeros((count, lanes), jnp.float32)]


def greet(view_count, scene_count, view, scene):
    barrier = pltpu.get_barrier_semaphore()
    for step in range(1, view_count):
        pl.semaphore_signal(
            barrier,
            inc=1,
            device_id=(lax.rem(view + step, view_count), scene),
            device_id_type=pl.DeviceIdType.MESH,
        )

    def to_scene(step, unused):
        pl.semaphore_signal(
            barrier,
            inc=1,
            device_id=(view, lax.rem(scene + step, scene_count)),
            device_id_type=pl.DeviceIdType.MESH,
        )
        return unused

    lax.fori_loop(1, scene_count, to_scene, 0)
    return barrier


def view_copy(outbox, inbox, sems, step, view, scene, view_count):
    peer = lax.rem(view + step, view_count)
    return pltpu.make_async_remote_copy(
        src_ref=outbox.at[peer],
        dst_ref=inbox.at[view],
        send_sem=sems[0].at[step],
        recv_sem=sems[1].at[step],
        device_id=(peer, scene),
        device_id_type=pl.DeviceIdType.MESH,
    )


def scene_copy(outbox, inbox, sems, step, view, scene, scene_count):
    peer = lax.rem(scene + step, scene_count)
    return pltpu.make_async_remote_copy(
        src_ref=outbox.at[peer],
        dst_ref=inbox.at[scene],
        send_sem=sems[0].at[step],
        recv_sem=sems[1].at[step],
        device_id=(view, peer),
        device_id_type=pl.DeviceIdType.MESH,
    )


def spread_kernel(
    view_count,
    scene_count,
    cameras,
    send,
    means,
    log_scales,
    rotations,
    opacity_logits,
    colour_coefs,
    incoming,
    view_out,
    view_in,
    blocks,
    scene_out,
    scene_in,
    view_send,
    view_recv,
    scene_send,
    scene_recv,
):
    view, scene = lax.axis_index("view"), lax.axis_index("scene")
    capacity = send.shape[1]
    block_count, lanes = means.shape[0], means.shape[2]
    barrier = greet(view_count, scene_count, view, scene)
    rows = project(
        camera_rows(cameras, block_count),
        *parameter_rows((means, log_scales, rotations, opacity_logits, colour_coefs), view_count),
    )
    for target in range(view_count):
        parts = []
        for block in range(block_count):
            at = target * block_count + block
            parts += [row[at : at + 1] for row in rows]
        spare = view_out.shape[1] - block_count * FEATURES
        view_out[target] = jnp.concatenate(fill(parts, spare, lanes), axis=0)
    pl.semaphore_wait(barrier, view_count + scene_count - 2)
    view_sems = (view_send, view_recv)
    for step in range(1, view_count):
        view_copy(view_out, view_in, view_sems, step, view, scene, view_count).start()
    view_in[view] = view_out[view]
    for step in range(1, view_count):
        view_copy(view_out, view_in, view_sems, step, view, scene, view_count).wait()
    for source in range(view_count):
        for block in range(block_count):
            blocks[source * block_count + block] = view_in[
                source, block * FEATURES : (block + 1) * FEATURES
            ]
    spare = scene_out.shape[1] - capacity * FEATURES

    def choose(peer, unused):
        parts = [blocks[jnp.maximum(send[peer, at], 0)] for at in range(capacity)]
        scene_out[peer] = jnp.concatenate(fill(parts, spare, lanes), axis=0)
        return unused

    def start(step, unused):
        choose(lax.rem(scene + step, scene_count), 0)
        scene_copy(scene_out, scene_in, scene_sems, step, view, scene, scene_count).start()
        return unused

    def place(source, box):
        for at in range(capacity):
            incoming[source * capacity + at] = box[at * FEATURES : (at + 1) * FEATURES]

    def finish(step, unused):
        scene_copy(scene_out, scene_in, scene_sems, step, view, scene, scene_count).wait()
        source = lax.rem(scene - step + scene_count, scene_count)
        place(source, scene_in[source])
        return unused

    scene_sems = (scene_send, scene_recv)
    lax.fori_loop(1, scene_count, start, 0)
    choose(scene, 0)
    place(scene, scene_out[scene])
    lax.fori_loop(1, scene_count, finish, 0)


def collect_kernel(
    view_count,
    scene_count,
    block_count,
    send,
    grads,
    own_grads,
    expo,
    scene_out,
    scene_in,
    view_out,
    view_in,
    scene_send,
    scene_recv,
    view_send,
    view_recv,
):
    view, scene = lax.axis_index("view"), lax.axis_index("scene")
    capacity = send.shape[1]
    lanes = grads.shape[2]
    barrier = greet(view_count, scene_count, view, scene)
    used = capacity * FEATURES
    spare = scene_out.shape[1] - used - 1

    def pack(peer, unused):
        parts = [grads[peer * capacity + at, 0:FEATURES] for at in range(capacity)]
        parts.append(grads[peer * capacity, FEATURES : FEATURES + 1])
        scene_out[peer] = jnp.concatenate(fill(parts, spare, lanes), axis=0)
        return unused

    lax.fori_loop(0, scene_count, pack, 0)
    pl.semaphore_wait(barrier, view_count + scene_count - 2)
    scene_sems = (scene_send, scene_recv)

    def start(step, unused):
        scene_copy(scene_out, scene_in, scene_sems, step, view, scene, scene_count).start()
        return unused

    def add(source, box, sums):
        sums = list(sums)
        for at in range(capacity):
            part = box[at * FEATURES : (at + 1) * FEATURES]
            home = send[source, at]
            for block in range(view_count * block_count):
                sums[block] = sums[block] + jnp.where(home == block, part, 0.0)
        sums[-1] = sums[-1] + box[used : used + 1]
        return tuple(sums)

    def finish(step, sums):
        scene_copy(scene_out, scene_in, scene_sems, step, view, scene, scene_count).wait()
        source = lax.rem(scene - step + scene_count, scene_count)
        return add(source, scene_in[source], sums)

    lax.fori_loop(1, scene_count, start, 0)
    empty = jnp.zeros((FEATURES, lanes), jnp.float32)
    sums = (empty,) * (view_count * block_count) + (jnp.zeros((1, lanes), jnp.float32),)
    sums = add(scene, scene_out[scene], sums)
    sums = lax.fori_loop(1, scene_count, finish, sums)
    expo[...] = sums[-1]
    spare = view_out.shape[1] - block_count * FEATURES
    for target in range(view_count):
        parts = list(sums[target * block_count : (target + 1) * block_count])
        view_out[target] = jnp.concatenate(fill(parts, spare, lanes), axis=0)
    view_sems = (view_send, view_recv)
    for step in range(1, view_count):
        view_copy(view_out, view_in, view_sems, step, view, scene, view_count).start()
    own_grads[view] = view_out[view]
    for step in range(1, view_count):
        view_copy(view_out, view_in, view_sems, step, view, scene, view_count).wait()
        source = lax.rem(view - step + view_count, view_count)
        own_grads[source] = view_in[source]


def unproject_kernel(
    cameras,
    own_grads,
    expo,
    means,
    log_scales,
    rotations,
    opacity_logits,
    colour_coefs,
    grad_means,
    grad_log_scales,
    grad_rotations,
    grad_opacity,
    grad_colour,
    grad_expo,
):
    view_count = cameras.shape[0]
    block_count = means.shape[0]
    cotangent = [
        jnp.concatenate(
            [
                own_grads[view, block * FEATURES + at : block * FEATURES + at + 1]
                for view in range(view_count)
                for block in range(block_count)
            ],
            axis=0,
        )
        for at in range(FEATURES)
    ]
    camera = camera_rows(cameras, block_count)
    pieces = parameter_rows(
        (means, log_scales, rotations, opacity_logits, colour_coefs), view_count
    )
    unproject = jax.vjp(functools.partial(project, camera), *pieces)[1]
    parts = unproject(cotangent)

    def store(ref, at, value):
        total = value[0:block_count]
        for view in range(1, view_count):
            total = total + value[view * block_count : (view + 1) * block_count]
        for block in range(block_count):
            ref[block, at : at + 1] = total[block : block + 1]

    for at in range(3):
        store(grad_means, at, parts[0][at])
        store(grad_log_scales, at, parts[1][at])
    for at in range(4):
        store(grad_rotations, at, parts[2][at])
    store(grad_opacity, 0, parts[3])
    for at in range(48):
        store(grad_colour, at, parts[4][at])
    grad_expo[...] = expo[:, 0:12]


def local(
    means,
    log_scales,
    rotations,
    opacity_logits,
    colour_coefs,
    cameras,
    exposure,
    target,
    tile_ids,
    send_list,
    pair_slots,
):
    view_count = lax.axis_size("view")
    scene_count = lax.axis_size("scene")
    own_params = (means, log_scales, rotations, opacity_logits, colour_coefs)
    block_count, lanes = means.shape[0], means.shape[2]
    capacity = send_list.shape[3]
    slots = scene_count * capacity
    send = send_list[0, 0]
    smem = pl.BlockSpec(memory_space=pltpu.SMEM)
    vmem = pl.BlockSpec(memory_space=pltpu.VMEM)
    view_box = (view_count, padded(block_count * FEATURES), lanes)
    scene_box = (scene_count, padded(capacity * FEATURES + 1), lanes)
    limit = 32 * 1024 * 1024
    incoming = pl.pallas_call(
        functools.partial(spread_kernel, view_count, scene_count),
        out_shape=jax.ShapeDtypeStruct((slots, FEATURES, lanes), jnp.float32),
        in_specs=[smem, smem] + [vmem] * 5,
        out_specs=vmem,
        scratch_shapes=[
            pltpu.VMEM(view_box, jnp.float32),
            pltpu.VMEM(view_box, jnp.float32),
            pltpu.VMEM((view_count * block_count, FEATURES, lanes), jnp.float32),
            pltpu.VMEM(scene_box, jnp.float32),
            pltpu.VMEM(scene_box, jnp.float32),
            pltpu.SemaphoreType.DMA((view_count,)),
            pltpu.SemaphoreType.DMA((view_count,)),
            pltpu.SemaphoreType.DMA((scene_count,)),
            pltpu.SemaphoreType.DMA((scene_count,)),
        ],
        compiler_params=pltpu.CompilerParams(
            collective_id=0, has_side_effects=True, vmem_limit_bytes=limit
        ),
        name="spread",
    )(cameras, send, *own_params)
    shown, grads = render(tile_ids, pair_slots[0], exposure, incoming, target)
    own_grads, expo = pl.pallas_call(
        functools.partial(collect_kernel, view_count, scene_count, block_count),
        out_shape=(
            jax.ShapeDtypeStruct(view_box, jnp.float32),
            jax.ShapeDtypeStruct((1, lanes), jnp.float32),
        ),
        in_specs=[smem, vmem],
        out_specs=(vmem, vmem),
        scratch_shapes=[
            pltpu.VMEM(scene_box, jnp.float32),
            pltpu.VMEM(scene_box, jnp.float32),
            pltpu.VMEM(view_box, jnp.float32),
            pltpu.VMEM(view_box, jnp.float32),
            pltpu.SemaphoreType.DMA((scene_count,)),
            pltpu.SemaphoreType.DMA((scene_count,)),
            pltpu.SemaphoreType.DMA((view_count,)),
            pltpu.SemaphoreType.DMA((view_count,)),
        ],
        compiler_params=pltpu.CompilerParams(
            collective_id=1, has_side_effects=True, vmem_limit_bytes=limit
        ),
        name="collect",
    )(send, grads)
    param_grads = pl.pallas_call(
        unproject_kernel,
        out_shape=tuple(jax.ShapeDtypeStruct(own.shape, jnp.float32) for own in own_params)
        + (jax.ShapeDtypeStruct((1, 12), jnp.float32),),
        in_specs=[smem] + [vmem] * 7,
        out_specs=(vmem,) * 6,
        compiler_params=pltpu.CompilerParams(vmem_limit_bytes=limit),
        name="unproject",
    )(cameras, own_grads, expo, *own_params)
    return (shown,) + tuple(param_grads)


def solution(mesh):
    return jax.shard_map(
        local,
        mesh=mesh,
        in_specs=(
            P(("view", "scene"), None, None),
            P(("view", "scene"), None, None),
            P(("view", "scene"), None, None),
            P(("view", "scene"), None, None),
            P(("view", "scene"), None, None),
            P(),
            P("view", None),
            P("view", "scene", None, None),
            P("view", "scene"),
            P("view", "scene", None, None),
            P("view", "scene", None),
        ),
        out_specs=(
            P("view", "scene", None, None),
            P(("view", "scene"), None, None),
            P(("view", "scene"), None, None),
            P(("view", "scene"), None, None),
            P(("view", "scene"), None, None),
            P(("view", "scene"), None, None),
            P("view", None),
        ),
        check_vma=False,
    )
```

```python
import functools

import jax
import jax.numpy as jnp
from jax import lax
from jax.experimental import pallas as pl
from jax.experimental.pallas import tpu as pltpu
from jax.sharding import PartitionSpec as P

PIX = 256
TILE_COLS = 32

FEATURES = 9

SH_ZERO = 0.28209479177387814
SH_ONE = 0.4886025119029199
SH_TWO = (
    1.0925484305920792,
    -1.0925484305920792,
    0.31539156525252005,
    -1.0925484305920792,
    0.5462742152960396,
)
SH_THREE = (
    -0.5900435899266435,
    2.890611442640554,
    -0.4570457994644658,
    0.3731763325901154,
    -0.4570457994644658,
    1.445305721320277,
    -0.5900435899266435,
)


def harmonics(dir_x, dir_y, dir_z):
    sq_x, sq_y, sq_z = (dir_x * dir_x, dir_y * dir_y, dir_z * dir_z)
    sh_basis = [
        SH_ZERO * jnp.ones_like(dir_x),
        -SH_ONE * dir_y,
        SH_ONE * dir_z,
        -SH_ONE * dir_x,
        SH_TWO[0] * dir_x * dir_y,
        SH_TWO[1] * dir_y * dir_z,
        SH_TWO[2] * (2.0 * sq_z - sq_x - sq_y),
        SH_TWO[3] * dir_x * dir_z,
        SH_TWO[4] * (sq_x - sq_y),
        SH_THREE[0] * dir_y * (3.0 * sq_x - sq_y),
        SH_THREE[1] * dir_x * dir_y * dir_z,
        SH_THREE[2] * dir_y * (4.0 * sq_z - sq_x - sq_y),
        SH_THREE[3] * dir_z * (2.0 * sq_z - 3.0 * sq_x - 3.0 * sq_y),
        SH_THREE[4] * dir_x * (4.0 * sq_z - sq_x - sq_y),
        SH_THREE[5] * dir_z * (sq_x - sq_y),
        SH_THREE[6] * dir_x * (sq_x - 3.0 * sq_y),
    ]
    return sh_basis


def project(camera, position, log_scales, rotations, opacity_logits, colour_coefs):
    rotation = [camera[0:3], camera[3:6], camera[6:9]]
    translation = camera[9:12]
    focal_x, focal_y, centre_x, centre_y = camera[12:16]
    view_pos = [
        rotation[row_at][0] * position[0]
        + rotation[row_at][1] * position[1]
        + rotation[row_at][2] * position[2]
        + translation[row_at]
        for row_at in range(3)
    ]
    inv_depth = 1.0 / view_pos[2]
    quat_w = rotations[0] + 3.0
    quat_x, quat_y, quat_z = (rotations[1], rotations[2], rotations[3])
    quat_norm = jnp.sqrt(quat_w * quat_w + quat_x * quat_x + quat_y * quat_y + quat_z * quat_z)
    quat_w, quat_x, quat_y, quat_z = (
        quat_w / quat_norm,
        quat_x / quat_norm,
        quat_y / quat_norm,
        quat_z / quat_norm,
    )
    spin_matrix = [
        [
            1.0 - 2.0 * (quat_y * quat_y + quat_z * quat_z),
            2.0 * (quat_x * quat_y - quat_w * quat_z),
            2.0 * (quat_x * quat_z + quat_w * quat_y),
        ],
        [
            2.0 * (quat_x * quat_y + quat_w * quat_z),
            1.0 - 2.0 * (quat_x * quat_x + quat_z * quat_z),
            2.0 * (quat_y * quat_z - quat_w * quat_x),
        ],
        [
            2.0 * (quat_x * quat_z - quat_w * quat_y),
            2.0 * (quat_y * quat_z + quat_w * quat_x),
            1.0 - 2.0 * (quat_x * quat_x + quat_y * quat_y),
        ],
    ]
    scales = [jnp.exp(row) for row in log_scales]
    world_frame = [
        [spin_matrix[row_at][col_at] * scales[col_at] for col_at in range(3)]
        for row_at in range(3)
    ]
    jacobian = [
        [
            focal_x * inv_depth * rotation[0][col_at]
            - focal_x * view_pos[0] * inv_depth * inv_depth * rotation[2][col_at]
            for col_at in range(3)
        ],
        [
            focal_y * inv_depth * rotation[1][col_at]
            - focal_y * view_pos[1] * inv_depth * inv_depth * rotation[2][col_at]
            for col_at in range(3)
        ],
    ]
    screen_frame = [
        [
            jacobian[row_at][0] * world_frame[0][col_at]
            + jacobian[row_at][1] * world_frame[1][col_at]
            + jacobian[row_at][2] * world_frame[2][col_at]
            for col_at in range(3)
        ]
        for row_at in range(2)
    ]
    sigma_xx = screen_frame[0][0] ** 2 + screen_frame[0][1] ** 2 + screen_frame[0][2] ** 2 + 0.3
    sigma_yy = screen_frame[1][0] ** 2 + screen_frame[1][1] ** 2 + screen_frame[1][2] ** 2 + 0.3
    sigma_xy = (
        screen_frame[0][0] * screen_frame[1][0]
        + screen_frame[0][1] * screen_frame[1][1]
        + screen_frame[0][2] * screen_frame[1][2]
    )
    determinant = sigma_xx * sigma_yy - sigma_xy * sigma_xy
    screen_x = focal_x * view_pos[0] * inv_depth + centre_x
    screen_y = focal_y * view_pos[1] * inv_depth + centre_y
    opacity = jax.nn.sigmoid(opacity_logits)
    eye_pos = [
        -(
            rotation[0][col_at] * translation[0]
            + rotation[1][col_at] * translation[1]
            + rotation[2][col_at] * translation[2]
        )
        for col_at in range(3)
    ]
    offsets = [position[col_at] - eye_pos[col_at] for col_at in range(3)]
    eye_dist = jnp.sqrt(offsets[0] ** 2 + offsets[1] ** 2 + offsets[2] ** 2)
    sh_basis = harmonics(offsets[0] / eye_dist, offsets[1] / eye_dist, offsets[2] / eye_dist)
    colour = []
    for channel in range(3):
        total = sh_basis[0] * colour_coefs[channel]
        for order in range(1, 16):
            total = total + sh_basis[order] * colour_coefs[3 * order + channel]
        colour.append(jnp.maximum(0.5 + total, 0.0))
    return [
        screen_x,
        screen_y,
        sigma_yy / determinant,
        -sigma_xy / determinant,
        sigma_xx / determinant,
        opacity,
    ] + colour


LOG2E = 1.4426950408889634


def split_pair(values):
    high = values.astype(jnp.bfloat16)
    low = (values - high.astype(jnp.float32)).astype(jnp.bfloat16)
    return jnp.concatenate([high, low], axis=1)


def render_kernel(
    tile_ids,
    slots,
    exposure,
    incoming,
    target,
    shown,
    grads,
    weight,
    ratio,
    weight_pair,
    expo_sum,
    before_mat,
    after_mat,
    powers,
    pixel_side,
):
    slot_count, tile_count = slots.shape
    lanes = incoming.shape[2]
    row_at = lax.broadcasted_iota(jnp.int32, (2 * lanes, 2 * lanes), 0) % lanes
    col_at = lax.broadcasted_iota(jnp.int32, (2 * lanes, 2 * lanes), 1)
    total = col_at >= lanes
    before_mat[...] = jnp.where(total | (row_at < col_at), 1.0, 0.0).astype(jnp.bfloat16)
    after_mat[...] = jnp.where(total | (row_at > col_at), 1.0, 0.0).astype(jnp.bfloat16)

    def monomials(power_at, pixel_at):
        side_x = (pixel_at % 16).astype(jnp.float32) - 7.5
        side_y = (pixel_at // 16).astype(jnp.float32) - 7.5
        one = jnp.ones_like(side_x)
        picks = [one, side_x, side_y, side_x * side_x, side_x * side_y, side_y * side_y]
        table = jnp.zeros_like(side_x)
        for at, pick in enumerate(picks):
            table = jnp.where(power_at == at, pick, table)
        return table.astype(jnp.bfloat16)

    powers[...] = monomials(
        lax.broadcasted_iota(jnp.int32, (8, PIX), 0), lax.broadcasted_iota(jnp.int32, (8, PIX), 1)
    )
    part_at = lax.broadcasted_iota(jnp.int32, (PIX, 32), 1)
    pixel_side[...] = monomials(
        jnp.where(part_at < 24, part_at % 8, 8), lax.broadcasted_iota(jnp.int32, (PIX, 32), 0)
    )
    grads[...] = jnp.zeros_like(grads)
    expo_sum[...] = jnp.zeros_like(expo_sum)
    mixing = [
        [exposure[0, 3 * i + j] + (1.0 if i == j else 0.0) for j in range(3)] for i in range(3)
    ]
    offset = [exposure[0, 9 + i] for i in range(3)]
    zero_rows = jnp.zeros((2, lanes), jnp.float32)

    def load(tile, at, centre_x, centre_y):
        block = incoming[slots[at, tile]]
        rows = [block[i : i + 1] for i in range(FEATURES)]
        rows[0] = rows[0] - centre_x
        rows[1] = rows[1] - centre_y
        return rows, block[6:9]

    def exponent(rows):
        pos_x, pos_y, con_a, con_b, con_c, opacity = rows[:6]
        lean_x = con_a * pos_x + con_b * pos_y
        lean_y = con_b * pos_x + con_c * pos_y
        base = jnp.log(opacity) - 0.5 * (pos_x * lean_x + pos_y * lean_y)
        whole = LOG2E * jnp.concatenate(
            [base, lean_x, lean_y, -0.5 * con_a, -con_b, -0.5 * con_c, zero_rows], axis=0
        )
        first = whole.astype(jnp.bfloat16).astype(jnp.float32)
        rest = whole - first
        second = rest.astype(jnp.bfloat16).astype(jnp.float32)
        return jnp.concatenate(
            [first, second, rest - second, jnp.zeros((8, lanes), jnp.float32)], axis=0
        ).astype(jnp.bfloat16)

    def one_tile(tile, live):
        tile_id = tile_ids[0, tile]
        centre_x = (16 * (tile_id % TILE_COLS) + 8).astype(jnp.float32)
        centre_y = (16 * (tile_id // TILE_COLS) + 8).astype(jnp.float32)
        carry = None
        shade = None
        for at in range(live):
            rows, colour = load(tile, at, centre_x, centre_y)
            alpha = jnp.exp2(
                jnp.dot(
                    pixel_side[...], exponent(rows), preferred_element_type=jnp.float32
                )
            )
            log_keep = jnp.log(1.0 - alpha)
            sums = jnp.dot(
                split_pair(log_keep), before_mat[...], preferred_element_type=jnp.float32
            )
            inside = sums[:, :lanes]
            if at > 0:
                inside = inside + carry
            if at + 1 < live:
                carry = sums[:, lanes:] if at == 0 else carry + sums[:, lanes:]
            seen = alpha * jnp.exp(inside)
            pair = split_pair(seen)
            weight[at] = seen
            ratio[at] = alpha * jnp.exp(-log_keep)
            weight_pair[at] = pair
            high = colour.astype(jnp.bfloat16).astype(jnp.float32)
            low = colour - high
            left = jnp.concatenate([high, low, zero_rows], axis=0)
            right = jnp.concatenate([high, jnp.zeros((5, lanes), jnp.float32)], axis=0)
            mixed = jnp.concatenate([left, right], axis=1).astype(jnp.bfloat16)
            term = lax.dot_general(
                mixed, pair, (((1,), (1,)), ((), ())), preferred_element_type=jnp.float32
            )
            shade = term if at == 0 else shade + term
        tone = [shade[i : i + 1] + shade[i + 3 : i + 4] for i in range(3)]
        image = [
            mixing[i][0] * tone[0] + mixing[i][1] * tone[1] + mixing[i][2] * tone[2] + offset[i]
            for i in range(3)
        ]
        for i in range(3):
            shown[i, pl.ds(tile, 1)] = image[i]
        miss = [image[i] - target[i, pl.ds(tile, 1)] for i in range(3)]
        expo_sum[...] += jnp.concatenate(
            [miss[i] * tone[j] for i in range(3) for j in range(3)] + miss, axis=0
        )
        back = jnp.concatenate(
            [
                mixing[0][j] * miss[0] + mixing[1][j] * miss[1] + mixing[2][j] * miss[2]
                for j in range(3)
            ],
            axis=0,
        )
        back_high = back.astype(jnp.bfloat16).astype(jnp.float32)
        back_low = back - back_high
        back_left = jnp.concatenate(
            [back_high, back_low, jnp.zeros((2, PIX), jnp.float32)], axis=0
        ).astype(jnp.bfloat16)
        back_side = jnp.transpose(
            jnp.concatenate(
                [back_high, back_high, back_low, jnp.zeros((7, PIX), jnp.float32)], axis=0
            )
        ).astype(jnp.bfloat16)
        carry = None
        for at in reversed(range(live)):
            rows, colour = load(tile, at, centre_x, centre_y)
            high = colour.astype(jnp.bfloat16).astype(jnp.float32)
            low = colour - high
            colour_side = jnp.concatenate(
                [high, low, high, jnp.zeros((7, lanes), jnp.float32)], axis=0
            ).astype(jnp.bfloat16)
            pull = jnp.dot(back_side, colour_side, preferred_element_type=jnp.float32)
            gain = weight[at] * pull
            sums = jnp.dot(split_pair(gain), after_mat[...], preferred_element_type=jnp.float32)
            behind = sums[:, :lanes]
            if at + 1 < live:
                behind = behind + carry
            if at > 0:
                carry = sums[:, lanes:] if at + 1 == live else carry + sums[:, lanes:]
            heat = gain - behind * ratio[at]
            moments = jnp.dot(powers[...], split_pair(heat), preferred_element_type=jnp.float32)
            moments = moments[:, :lanes] + moments[:, lanes:]
            tint = jnp.dot(back_left, weight_pair[at], preferred_element_type=jnp.float32)
            tint = tint[:, :lanes] + tint[:, lanes:]
            tint = tint[0:3] + tint[3:6]
            pos_x, pos_y, con_a, con_b, con_c, opacity = rows[:6]
            m_one, m_x, m_y, m_xx, m_xy, m_yy = [moments[i : i + 1] for i in range(6)]
            d_x = m_x - pos_x * m_one
            d_y = m_y - pos_y * m_one
            d_xx = m_xx - pos_x * (m_x + d_x)
            d_xy = m_xy - pos_x * m_y - pos_y * d_x
            d_yy = m_yy - pos_y * (m_y + d_y)
            grads[slots[at, tile], 0:FEATURES] += jnp.concatenate(
                [
                    con_a * d_x + con_b * d_y,
                    con_b * d_x + con_c * d_y,
                    -0.5 * d_xx,
                    -d_xy,
                    -0.5 * d_yy,
                    m_one / opacity,
                    tint,
                ],
                axis=0,
            )

    def tile_step(tile, unused):
        live = jnp.int32(0)
        for at in range(slot_count):
            live = live + jnp.where(slots[at, tile] >= 0, 1, 0)
        for number in range(1, slot_count + 1):
            pl.when(live == number)(functools.partial(one_tile, tile, number))
        return unused

    lax.fori_loop(0, tile_count, tile_step, 0)
    sums = jnp.sum(expo_sum[...], axis=1, keepdims=True)
    lane_at = lax.broadcasted_iota(jnp.int32, (12, lanes), 1)
    row_at = lax.broadcasted_iota(jnp.int32, (12, lanes), 0)
    spread = jnp.sum(jnp.where(lane_at == row_at, sums, 0.0), axis=0, keepdims=True)
    grads[:, FEATURES : FEATURES + 1] = jnp.broadcast_to(spread[None], (grads.shape[0], 1, lanes))


def render(tile_ids, slots, exposure, incoming, target):
    slot_count = slots.shape[0]
    lanes = incoming.shape[2]
    smem = pl.BlockSpec(memory_space=pltpu.SMEM)
    vmem = pl.BlockSpec(memory_space=pltpu.VMEM)
    return pl.pallas_call(
        render_kernel,
        out_shape=(
            jax.ShapeDtypeStruct(target.shape, jnp.float32),
            jax.ShapeDtypeStruct((incoming.shape[0], FEATURES + 1, lanes), jnp.float32),
        ),
        in_specs=[smem, smem, smem, vmem, vmem],
        out_specs=(vmem, vmem),
        scratch_shapes=[
            pltpu.VMEM((slot_count, PIX, lanes), jnp.float32),
            pltpu.VMEM((slot_count, PIX, lanes), jnp.float32),
            pltpu.VMEM((slot_count, PIX, 2 * lanes), jnp.bfloat16),
            pltpu.VMEM((12, PIX), jnp.float32),
            pltpu.VMEM((2 * lanes, 2 * lanes), jnp.bfloat16),
            pltpu.VMEM((2 * lanes, 2 * lanes), jnp.bfloat16),
            pltpu.VMEM((8, PIX), jnp.bfloat16),
            pltpu.VMEM((PIX, 32), jnp.bfloat16),
        ],
        compiler_params=pltpu.CompilerParams(vmem_limit_bytes=32 * 1024 * 1024),
        name="render",
    )(tile_ids, slots, exposure, incoming, target)


def padded(rows):
    return (rows + 7) // 8 * 8


def camera_rows(cameras, block_count):
    view_count = cameras.shape[0]
    shape = (view_count * block_count, 128)
    view_at = lax.broadcasted_iota(jnp.int32, shape, 0) // block_count
    entries = []
    for entry in range(16):
        value = jnp.full(shape, cameras[0, entry])
        for view in range(1, view_count):
            value = jnp.where(view_at == view, cameras[view, entry], value)
        entries.append(value)
    return entries


def parameter_rows(refs, view_count):
    block_count = refs[0].shape[1]

    def row(ref, at):
        own = [ref[block, at : at + 1] for block in range(block_count)]
        return jnp.concatenate(own * view_count, axis=0)

    def plane(ref, at):
        return jnp.concatenate([ref[at]] * view_count, axis=0)

    means, log_scales, rotations, opacity_logits, colour_coefs = refs
    return (
        [plane(means, at) for at in range(3)],
        [plane(log_scales, at) for at in range(3)],
        [row(rotations, at) for at in range(4)],
        row(opacity_logits, 0),
        [row(colour_coefs, at) for at in range(48)],
    )


def fill(rows, count, lanes):
    return rows if count == 0 else rows + [jnp.zeros((count, lanes), jnp.float32)]


def greet(view_count, scene_count, view, scene):
    barrier = pltpu.get_barrier_semaphore()
    for step in range(1, view_count):
        pl.semaphore_signal(
            barrier,
            inc=1,
            device_id=(lax.rem(view + step, view_count), scene),
            device_id_type=pl.DeviceIdType.MESH,
        )

    def to_scene(step, unused):
        pl.semaphore_signal(
            barrier,
            inc=1,
            device_id=(view, lax.rem(scene + step, scene_count)),
            device_id_type=pl.DeviceIdType.MESH,
        )
        return unused

    lax.fori_loop(1, scene_count, to_scene, 0)
    return barrier


def view_copy(outbox, inbox, sems, step, view, scene, view_count):
    peer = lax.rem(view + step, view_count)
    return pltpu.make_async_remote_copy(
        src_ref=outbox.at[peer],
        dst_ref=inbox.at[view],
        send_sem=sems[0].at[step],
        recv_sem=sems[1].at[step],
        device_id=(peer, scene),
        device_id_type=pl.DeviceIdType.MESH,
    )


def scene_copy(outbox, inbox, sems, step, view, scene, scene_count):
    peer = lax.rem(scene + step, scene_count)
    return pltpu.make_async_remote_copy(
        src_ref=outbox.at[peer],
        dst_ref=inbox.at[scene],
        send_sem=sems[0].at[step],
        recv_sem=sems[1].at[step],
        device_id=(view, peer),
        device_id_type=pl.DeviceIdType.MESH,
    )


def spread_kernel(
    view_count,
    scene_count,
    cameras,
    send,
    means,
    log_scales,
    rotations,
    opacity_logits,
    colour_coefs,
    incoming,
    view_out,
    view_in,
    blocks,
    scene_out,
    scene_in,
    view_send,
    view_recv,
    scene_send,
    scene_recv,
):
    view, scene = lax.axis_index("view"), lax.axis_index("scene")
    capacity = send.shape[0]
    block_count, lanes = means.shape[1], means.shape[2]
    barrier = greet(view_count, scene_count, view, scene)
    rows = project(
        camera_rows(cameras, block_count),
        *parameter_rows((means, log_scales, rotations, opacity_logits, colour_coefs), view_count),
    )
    for target in range(view_count):
        parts = []
        for block in range(block_count):
            at = target * block_count + block
            parts += [row[at : at + 1] for row in rows]
        spare = view_out.shape[1] - block_count * FEATURES
        view_out[target] = jnp.concatenate(fill(parts, spare, lanes), axis=0)
    pl.semaphore_wait(barrier, view_count + scene_count - 2)
    view_sems = (view_send, view_recv)
    for step in range(1, view_count):
        view_copy(view_out, view_in, view_sems, step, view, scene, view_count).start()
    view_in[view] = view_out[view]
    for step in range(1, view_count):
        view_copy(view_out, view_in, view_sems, step, view, scene, view_count).wait()
    for source in range(view_count):
        for block in range(block_count):
            blocks[source * block_count + block] = view_in[
                source, block * FEATURES : (block + 1) * FEATURES
            ]
    spare = scene_out.shape[1] - capacity * FEATURES

    def choose(peer, unused):
        parts = [blocks[jnp.maximum(send[at, peer], 0)] for at in range(capacity)]
        scene_out[peer] = jnp.concatenate(fill(parts, spare, lanes), axis=0)
        return unused

    def start(step, unused):
        choose(lax.rem(scene + step, scene_count), 0)
        scene_copy(scene_out, scene_in, scene_sems, step, view, scene, scene_count).start()
        return unused

    def place(source, box):
        for at in range(capacity):
            incoming[source * capacity + at] = box[at * FEATURES : (at + 1) * FEATURES]

    def finish(step, unused):
        scene_copy(scene_out, scene_in, scene_sems, step, view, scene, scene_count).wait()
        source = lax.rem(scene - step + scene_count, scene_count)
        place(source, scene_in[source])
        return unused

    scene_sems = (scene_send, scene_recv)
    lax.fori_loop(1, scene_count, start, 0)
    choose(scene, 0)
    place(scene, scene_out[scene])
    lax.fori_loop(1, scene_count, finish, 0)


def collect_kernel(
    view_count,
    scene_count,
    block_count,
    send,
    grads,
    own_grads,
    expo,
    scene_out,
    scene_in,
    view_out,
    view_in,
    scene_send,
    scene_recv,
    view_send,
    view_recv,
):
    view, scene = lax.axis_index("view"), lax.axis_index("scene")
    capacity = send.shape[0]
    lanes = grads.shape[2]
    barrier = greet(view_count, scene_count, view, scene)
    used = capacity * FEATURES
    spare = scene_out.shape[1] - used - 1

    def pack(peer, unused):
        parts = [grads[peer * capacity + at, 0:FEATURES] for at in range(capacity)]
        parts.append(grads[peer * capacity, FEATURES : FEATURES + 1])
        scene_out[peer] = jnp.concatenate(fill(parts, spare, lanes), axis=0)
        return unused

    lax.fori_loop(0, scene_count, pack, 0)
    pl.semaphore_wait(barrier, view_count + scene_count - 2)
    scene_sems = (scene_send, scene_recv)

    def start(step, unused):
        scene_copy(scene_out, scene_in, scene_sems, step, view, scene, scene_count).start()
        return unused

    def add(source, box, sums):
        sums = list(sums)
        for at in range(capacity):
            part = box[at * FEATURES : (at + 1) * FEATURES]
            home = send[at, source]
            for block in range(view_count * block_count):
                sums[block] = sums[block] + jnp.where(home == block, part, 0.0)
        sums[-1] = sums[-1] + box[used : used + 1]
        return tuple(sums)

    def finish(step, sums):
        scene_copy(scene_out, scene_in, scene_sems, step, view, scene, scene_count).wait()
        source = lax.rem(scene - step + scene_count, scene_count)
        return add(source, scene_in[source], sums)

    lax.fori_loop(1, scene_count, start, 0)
    empty = jnp.zeros((FEATURES, lanes), jnp.float32)
    sums = (empty,) * (view_count * block_count) + (jnp.zeros((1, lanes), jnp.float32),)
    sums = add(scene, scene_out[scene], sums)
    sums = lax.fori_loop(1, scene_count, finish, sums)
    expo[...] = sums[-1]
    spare = view_out.shape[1] - block_count * FEATURES
    for target in range(view_count):
        parts = list(sums[target * block_count : (target + 1) * block_count])
        view_out[target] = jnp.concatenate(fill(parts, spare, lanes), axis=0)
    view_sems = (view_send, view_recv)
    for step in range(1, view_count):
        view_copy(view_out, view_in, view_sems, step, view, scene, view_count).start()
    own_grads[view] = view_out[view]
    for step in range(1, view_count):
        view_copy(view_out, view_in, view_sems, step, view, scene, view_count).wait()
        source = lax.rem(view - step + view_count, view_count)
        own_grads[source] = view_in[source]


def unproject_kernel(
    cameras,
    own_grads,
    expo,
    means,
    log_scales,
    rotations,
    opacity_logits,
    colour_coefs,
    grad_means,
    grad_log_scales,
    grad_rotations,
    grad_opacity,
    grad_colour,
    grad_expo,
):
    view_count = cameras.shape[0]
    block_count = means.shape[1]
    cotangent = [
        jnp.concatenate(
            [
                own_grads[view, block * FEATURES + at : block * FEATURES + at + 1]
                for view in range(view_count)
                for block in range(block_count)
            ],
            axis=0,
        )
        for at in range(FEATURES)
    ]
    camera = camera_rows(cameras, block_count)
    pieces = parameter_rows(
        (means, log_scales, rotations, opacity_logits, colour_coefs), view_count
    )
    unproject = jax.vjp(functools.partial(project, camera), *pieces)[1]
    parts = unproject(cotangent)

    def over_views(value):
        total = value[0:block_count]
        for view in range(1, view_count):
            total = total + value[view * block_count : (view + 1) * block_count]
        return total

    def store(ref, at, value):
        total = over_views(value)
        for block in range(block_count):
            ref[block, at : at + 1] = total[block : block + 1]

    for at in range(3):
        grad_means[at] = over_views(parts[0][at])
        grad_log_scales[at] = over_views(parts[1][at])
    for at in range(4):
        store(grad_rotations, at, parts[2][at])
    store(grad_opacity, 0, parts[3])
    for at in range(48):
        store(grad_colour, at, parts[4][at])
    grad_expo[...] = expo[:, 0:12]


def local(
    means,
    log_scales,
    rotations,
    opacity_logits,
    colour_coefs,
    cameras,
    exposure,
    target,
    tile_ids,
    send_list,
    pair_slots,
):
    view_count = lax.axis_size("view")
    scene_count = lax.axis_size("scene")
    own_params = (
        jnp.transpose(means, (1, 0, 2)),
        jnp.transpose(log_scales, (1, 0, 2)),
        rotations,
        opacity_logits,
        colour_coefs,
    )
    block_count, lanes = means.shape[0], means.shape[2]
    capacity = send_list.shape[3]
    slots = scene_count * capacity
    send = send_list[0, 0].T
    smem = pl.BlockSpec(memory_space=pltpu.SMEM)
    vmem = pl.BlockSpec(memory_space=pltpu.VMEM)
    view_box = (view_count, padded(block_count * FEATURES), lanes)
    scene_box = (scene_count, padded(capacity * FEATURES + 1), lanes)
    limit = 32 * 1024 * 1024
    incoming = pl.pallas_call(
        functools.partial(spread_kernel, view_count, scene_count),
        out_shape=jax.ShapeDtypeStruct((slots, FEATURES, lanes), jnp.float32),
        in_specs=[smem, smem] + [vmem] * 5,
        out_specs=vmem,
        scratch_shapes=[
            pltpu.VMEM(view_box, jnp.float32),
            pltpu.VMEM(view_box, jnp.float32),
            pltpu.VMEM((view_count * block_count, FEATURES, lanes), jnp.float32),
            pltpu.VMEM(scene_box, jnp.float32),
            pltpu.VMEM(scene_box, jnp.float32),
            pltpu.SemaphoreType.DMA((view_count,)),
            pltpu.SemaphoreType.DMA((view_count,)),
            pltpu.SemaphoreType.DMA((scene_count,)),
            pltpu.SemaphoreType.DMA((scene_count,)),
        ],
        compiler_params=pltpu.CompilerParams(
            collective_id=0, has_side_effects=True, vmem_limit_bytes=limit
        ),
        name="spread",
    )(cameras, send, *own_params)
    shown, grads = render(
        tile_ids, pair_slots[0].T, exposure, incoming, jnp.transpose(target[0], (1, 0, 2))
    )
    own_grads, expo = pl.pallas_call(
        functools.partial(collect_kernel, view_count, scene_count, block_count),
        out_shape=(
            jax.ShapeDtypeStruct(view_box, jnp.float32),
            jax.ShapeDtypeStruct((1, lanes), jnp.float32),
        ),
        in_specs=[smem, vmem],
        out_specs=(vmem, vmem),
        scratch_shapes=[
            pltpu.VMEM(scene_box, jnp.float32),
            pltpu.VMEM(scene_box, jnp.float32),
            pltpu.VMEM(view_box, jnp.float32),
            pltpu.VMEM(view_box, jnp.float32),
            pltpu.SemaphoreType.DMA((scene_count,)),
            pltpu.SemaphoreType.DMA((scene_count,)),
            pltpu.SemaphoreType.DMA((view_count,)),
            pltpu.SemaphoreType.DMA((view_count,)),
        ],
        compiler_params=pltpu.CompilerParams(
            collective_id=1, has_side_effects=True, vmem_limit_bytes=limit
        ),
        name="collect",
    )(send, grads)
    param_grads = pl.pallas_call(
        unproject_kernel,
        out_shape=tuple(jax.ShapeDtypeStruct(own.shape, jnp.float32) for own in own_params)
        + (jax.ShapeDtypeStruct((1, 12), jnp.float32),),
        in_specs=[smem] + [vmem] * 7,
        out_specs=(vmem,) * 6,
        compiler_params=pltpu.CompilerParams(vmem_limit_bytes=limit),
        name="unproject",
    )(cameras, own_grads, expo, *own_params)
    return (
        jnp.transpose(shown, (1, 0, 2))[None],
        jnp.transpose(param_grads[0], (1, 0, 2)),
        jnp.transpose(param_grads[1], (1, 0, 2)),
    ) + tuple(param_grads[2:])


def solution(mesh):
    return jax.shard_map(
        local,
        mesh=mesh,
        in_specs=(
            P(("view", "scene"), None, None),
            P(("view", "scene"), None, None),
            P(("view", "scene"), None, None),
            P(("view", "scene"), None, None),
            P(("view", "scene"), None, None),
            P(),
            P("view", None),
            P("view", "scene", None, None),
            P("view", "scene"),
            P("view", "scene", None, None),
            P("view", "scene", None),
        ),
        out_specs=(
            P("view", "scene", None, None),
            P(("view", "scene"), None, None),
            P(("view", "scene"), None, None),
            P(("view", "scene"), None, None),
            P(("view", "scene"), None, None),
            P(("view", "scene"), None, None),
            P("view", None),
        ),
        check_vma=False,
    )
```

```python
import functools

import jax
import jax.numpy as jnp
from jax import lax
from jax.experimental import pallas as pl
from jax.experimental.pallas import tpu as pltpu
from jax.sharding import PartitionSpec as P

PIX = 256
TILE_COLS = 32

FEATURES = 9

SH_ZERO = 0.28209479177387814
SH_ONE = 0.4886025119029199
SH_TWO = (
    1.0925484305920792,
    -1.0925484305920792,
    0.31539156525252005,
    -1.0925484305920792,
    0.5462742152960396,
)
SH_THREE = (
    -0.5900435899266435,
    2.890611442640554,
    -0.4570457994644658,
    0.3731763325901154,
    -0.4570457994644658,
    1.445305721320277,
    -0.5900435899266435,
)


def harmonics(dir_x, dir_y, dir_z):
    sq_x, sq_y, sq_z = (dir_x * dir_x, dir_y * dir_y, dir_z * dir_z)
    sh_basis = [
        SH_ZERO * jnp.ones_like(dir_x),
        -SH_ONE * dir_y,
        SH_ONE * dir_z,
        -SH_ONE * dir_x,
        SH_TWO[0] * dir_x * dir_y,
        SH_TWO[1] * dir_y * dir_z,
        SH_TWO[2] * (2.0 * sq_z - sq_x - sq_y),
        SH_TWO[3] * dir_x * dir_z,
        SH_TWO[4] * (sq_x - sq_y),
        SH_THREE[0] * dir_y * (3.0 * sq_x - sq_y),
        SH_THREE[1] * dir_x * dir_y * dir_z,
        SH_THREE[2] * dir_y * (4.0 * sq_z - sq_x - sq_y),
        SH_THREE[3] * dir_z * (2.0 * sq_z - 3.0 * sq_x - 3.0 * sq_y),
        SH_THREE[4] * dir_x * (4.0 * sq_z - sq_x - sq_y),
        SH_THREE[5] * dir_z * (sq_x - sq_y),
        SH_THREE[6] * dir_x * (sq_x - 3.0 * sq_y),
    ]
    return sh_basis


def project(camera, position, log_scales, rotations, opacity_logits, colour_coefs):
    rotation = [camera[0:3], camera[3:6], camera[6:9]]
    translation = camera[9:12]
    focal_x, focal_y, centre_x, centre_y = camera[12:16]
    view_pos = [
        rotation[row_at][0] * position[0]
        + rotation[row_at][1] * position[1]
        + rotation[row_at][2] * position[2]
        + translation[row_at]
        for row_at in range(3)
    ]
    inv_depth = 1.0 / view_pos[2]
    quat_w = rotations[0] + 3.0
    quat_x, quat_y, quat_z = (rotations[1], rotations[2], rotations[3])
    quat_norm = jnp.sqrt(quat_w * quat_w + quat_x * quat_x + quat_y * quat_y + quat_z * quat_z)
    quat_w, quat_x, quat_y, quat_z = (
        quat_w / quat_norm,
        quat_x / quat_norm,
        quat_y / quat_norm,
        quat_z / quat_norm,
    )
    spin_matrix = [
        [
            1.0 - 2.0 * (quat_y * quat_y + quat_z * quat_z),
            2.0 * (quat_x * quat_y - quat_w * quat_z),
            2.0 * (quat_x * quat_z + quat_w * quat_y),
        ],
        [
            2.0 * (quat_x * quat_y + quat_w * quat_z),
            1.0 - 2.0 * (quat_x * quat_x + quat_z * quat_z),
            2.0 * (quat_y * quat_z - quat_w * quat_x),
        ],
        [
            2.0 * (quat_x * quat_z - quat_w * quat_y),
            2.0 * (quat_y * quat_z + quat_w * quat_x),
            1.0 - 2.0 * (quat_x * quat_x + quat_y * quat_y),
        ],
    ]
    scales = [jnp.exp(row) for row in log_scales]
    world_frame = [
        [spin_matrix[row_at][col_at] * scales[col_at] for col_at in range(3)]
        for row_at in range(3)
    ]
    jacobian = [
        [
            focal_x * inv_depth * rotation[0][col_at]
            - focal_x * view_pos[0] * inv_depth * inv_depth * rotation[2][col_at]
            for col_at in range(3)
        ],
        [
            focal_y * inv_depth * rotation[1][col_at]
            - focal_y * view_pos[1] * inv_depth * inv_depth * rotation[2][col_at]
            for col_at in range(3)
        ],
    ]
    screen_frame = [
        [
            jacobian[row_at][0] * world_frame[0][col_at]
            + jacobian[row_at][1] * world_frame[1][col_at]
            + jacobian[row_at][2] * world_frame[2][col_at]
            for col_at in range(3)
        ]
        for row_at in range(2)
    ]
    sigma_xx = screen_frame[0][0] ** 2 + screen_frame[0][1] ** 2 + screen_frame[0][2] ** 2 + 0.3
    sigma_yy = screen_frame[1][0] ** 2 + screen_frame[1][1] ** 2 + screen_frame[1][2] ** 2 + 0.3
    sigma_xy = (
        screen_frame[0][0] * screen_frame[1][0]
        + screen_frame[0][1] * screen_frame[1][1]
        + screen_frame[0][2] * screen_frame[1][2]
    )
    determinant = sigma_xx * sigma_yy - sigma_xy * sigma_xy
    screen_x = focal_x * view_pos[0] * inv_depth + centre_x
    screen_y = focal_y * view_pos[1] * inv_depth + centre_y
    opacity = jax.nn.sigmoid(opacity_logits)
    eye_pos = [
        -(
            rotation[0][col_at] * translation[0]
            + rotation[1][col_at] * translation[1]
            + rotation[2][col_at] * translation[2]
        )
        for col_at in range(3)
    ]
    offsets = [position[col_at] - eye_pos[col_at] for col_at in range(3)]
    eye_dist = jnp.sqrt(offsets[0] ** 2 + offsets[1] ** 2 + offsets[2] ** 2)
    sh_basis = harmonics(offsets[0] / eye_dist, offsets[1] / eye_dist, offsets[2] / eye_dist)
    colour = []
    for channel in range(3):
        total = sh_basis[0] * colour_coefs[channel]
        for order in range(1, 16):
            total = total + sh_basis[order] * colour_coefs[3 * order + channel]
        colour.append(jnp.maximum(0.5 + total, 0.0))
    return [
        screen_x,
        screen_y,
        sigma_yy / determinant,
        -sigma_xy / determinant,
        sigma_xx / determinant,
        opacity,
    ] + colour


LOG2E = 1.4426950408889634


def split_pair(values):
    high = values.astype(jnp.bfloat16)
    low = (values - high.astype(jnp.float32)).astype(jnp.bfloat16)
    return jnp.concatenate([high, low], axis=1)


def render_kernel(
    tile_ids,
    slots,
    exposure,
    incoming,
    target,
    shown,
    grads,
    weight,
    ratio,
    weight_pair,
    expo_sum,
    before_mat,
    after_mat,
):
    slot_count, tile_count = slots.shape
    lanes = incoming.shape[2]
    row_at = lax.broadcasted_iota(jnp.int32, (2 * lanes, 2 * lanes), 0) % lanes
    col_at = lax.broadcasted_iota(jnp.int32, (2 * lanes, 2 * lanes), 1)
    total = col_at >= lanes
    before_mat[...] = jnp.where(total | (row_at < col_at), 1.0, 0.0).astype(jnp.bfloat16)
    after_mat[...] = jnp.where(total | (row_at > col_at), 1.0, 0.0).astype(jnp.bfloat16)
    grads[...] = jnp.zeros_like(grads)
    expo_sum[...] = jnp.zeros_like(expo_sum)
    mixing = [
        [exposure[0, 3 * i + j] + (1.0 if i == j else 0.0) for j in range(3)] for i in range(3)
    ]
    offset = [exposure[0, 9 + i] for i in range(3)]
    local_x = [
        lax.broadcasted_iota(jnp.int32, (8, lanes), 0).astype(jnp.float32) + (8.0 * half - 7.5)
        for half in range(2)
    ]
    zero_rows = jnp.zeros((2, lanes), jnp.float32)

    def load(tile, at, centre_x, centre_y):
        block = incoming[slots[at, tile]]
        rows = [block[i : i + 1] for i in range(FEATURES)]
        rows[0] = rows[0] - centre_x
        rows[1] = rows[1] - centre_y
        return rows, block[6:9]

    def moments(heat):
        flat, tilt, bend = [], [], []
        for half in range(2):
            sums = None
            for line in range(PIX // 32):
                far = PIX // 16 - 1 - line
                first = heat[16 * line + 8 * half : 16 * line + 8 * half + 8]
                last = heat[16 * far + 8 * half : 16 * far + 8 * half + 8]
                both, apart = last + first, last - first
                side = far - 7.5
                terms = (both, apart * side, both * (side * side))
                sums = terms if sums is None else [a + b for a, b in zip(sums, terms)]
            flat.append(sums[0])
            tilt.append(sums[1])
            bend.append(sums[2])
        slide = [part * side for part, side in zip(flat, local_x)]
        fields = [
            flat[0] + flat[1],
            slide[0] + slide[1],
            tilt[0] + tilt[1],
            slide[0] * local_x[0] + slide[1] * local_x[1],
            tilt[0] * local_x[0] + tilt[1] * local_x[1],
            bend[0] + bend[1],
        ]
        return [jnp.sum(field, axis=0, keepdims=True) for field in fields]

    def one_tile(tile, live):
        tile_id = tile_ids[0, tile]
        centre_x = (16 * (tile_id % TILE_COLS) + 8).astype(jnp.float32)
        centre_y = (16 * (tile_id // TILE_COLS) + 8).astype(jnp.float32)
        carry = None
        shade = None
        for at in range(live):
            rows, colour = load(tile, at, centre_x, centre_y)
            wide = [jnp.broadcast_to(row, (8, lanes)) for row in rows[:6]]
            gap_x = [side - wide[0] for side in local_x]
            scaled_a = wide[2] * (-0.5 * LOG2E)
            scaled_b = wide[3] * (-LOG2E)
            scaled_c = wide[4] * (-0.5 * LOG2E)
            part_x = [scaled_a * gap * gap for gap in gap_x]
            pieces = []
            for line in range(PIX // 16):
                gap_y = (line - 7.5) - wide[1]
                part_y = scaled_c * gap_y * gap_y
                slope = scaled_b * gap_y
                for half in range(2):
                    pieces.append(
                        wide[5] * jnp.exp2(part_x[half] + gap_x[half] * slope + part_y)
                    )
            alpha = jnp.concatenate(pieces, axis=0)
            log_keep = jnp.log(1.0 - alpha)
            width = 2 * lanes if at + 1 < live else lanes
            sums = jnp.dot(
                split_pair(log_keep), before_mat[:, :width], preferred_element_type=jnp.float32
            )
            inside = sums[:, :lanes]
            if at > 0:
                inside = inside + carry
            if at + 1 < live:
                carry = sums[:, lanes:] if at == 0 else carry + sums[:, lanes:]
            seen = alpha * jnp.exp(inside)
            pair = split_pair(seen)
            weight[at] = seen
            ratio[at] = alpha * jnp.exp(-log_keep)
            weight_pair[at] = pair
            high = colour.astype(jnp.bfloat16).astype(jnp.float32)
            low = colour - high
            left = jnp.concatenate([high, low, zero_rows], axis=0)
            right = jnp.concatenate([high, jnp.zeros((5, lanes), jnp.float32)], axis=0)
            mixed = jnp.concatenate([left, right], axis=1).astype(jnp.bfloat16)
            term = lax.dot_general(
                mixed, pair, (((1,), (1,)), ((), ())), preferred_element_type=jnp.float32
            )
            shade = term if at == 0 else shade + term
        tone = [shade[i : i + 1] + shade[i + 3 : i + 4] for i in range(3)]
        image = [
            mixing[i][0] * tone[0] + mixing[i][1] * tone[1] + mixing[i][2] * tone[2] + offset[i]
            for i in range(3)
        ]
        for i in range(3):
            shown[i, pl.ds(tile, 1)] = image[i]
        miss = [image[i] - target[i, pl.ds(tile, 1)] for i in range(3)]
        expo_sum[...] += jnp.concatenate(
            [miss[i] * tone[j] for i in range(3) for j in range(3)] + miss, axis=0
        )
        back = jnp.concatenate(
            [
                mixing[0][j] * miss[0] + mixing[1][j] * miss[1] + mixing[2][j] * miss[2]
                for j in range(3)
            ],
            axis=0,
        )
        back_high = back.astype(jnp.bfloat16).astype(jnp.float32)
        back_low = back - back_high
        back_left = jnp.concatenate(
            [back_high, back_low, jnp.zeros((2, PIX), jnp.float32)], axis=0
        ).astype(jnp.bfloat16)
        back_side = jnp.transpose(
            jnp.concatenate(
                [back_high, back_high, back_low, jnp.zeros((7, PIX), jnp.float32)], axis=0
            )
        ).astype(jnp.bfloat16)
        carry = None
        for at in reversed(range(live)):
            rows, colour = load(tile, at, centre_x, centre_y)
            high = colour.astype(jnp.bfloat16).astype(jnp.float32)
            low = colour - high
            colour_side = jnp.concatenate(
                [high, low, high, jnp.zeros((7, lanes), jnp.float32)], axis=0
            ).astype(jnp.bfloat16)
            pull = jnp.dot(back_side, colour_side, preferred_element_type=jnp.float32)
            gain = weight[at] * pull
            width = 2 * lanes if at > 0 else lanes
            sums = jnp.dot(
                split_pair(gain), after_mat[:, :width], preferred_element_type=jnp.float32
            )
            behind = sums[:, :lanes]
            if at + 1 < live:
                behind = behind + carry
            if at > 0:
                carry = sums[:, lanes:] if at + 1 == live else carry + sums[:, lanes:]
            heat = gain - behind * ratio[at]
            tint = jnp.dot(back_left, weight_pair[at], preferred_element_type=jnp.float32)
            tint = tint[:, :lanes] + tint[:, lanes:]
            tint = tint[0:3] + tint[3:6]
            pos_x, pos_y, con_a, con_b, con_c, opacity = rows[:6]
            m_one, m_x, m_y, m_xx, m_xy, m_yy = moments(heat)
            d_x = m_x - pos_x * m_one
            d_y = m_y - pos_y * m_one
            d_xx = m_xx - pos_x * (m_x + d_x)
            d_xy = m_xy - pos_x * m_y - pos_y * d_x
            d_yy = m_yy - pos_y * (m_y + d_y)
            grads[slots[at, tile], 0:FEATURES] += jnp.concatenate(
                [
                    con_a * d_x + con_b * d_y,
                    con_b * d_x + con_c * d_y,
                    -0.5 * d_xx,
                    -d_xy,
                    -0.5 * d_yy,
                    m_one / opacity,
                    tint,
                ],
                axis=0,
            )

    def tile_step(tile, unused):
        live = jnp.int32(0)
        for at in range(slot_count):
            live = live + jnp.where(slots[at, tile] >= 0, 1, 0)
        for number in range(1, slot_count + 1):
            pl.when(live == number)(functools.partial(one_tile, tile, number))
        return unused

    lax.fori_loop(0, tile_count, tile_step, 0)
    sums = jnp.sum(expo_sum[...], axis=1, keepdims=True)
    lane_at = lax.broadcasted_iota(jnp.int32, (12, lanes), 1)
    row_at = lax.broadcasted_iota(jnp.int32, (12, lanes), 0)
    spread = jnp.sum(jnp.where(lane_at == row_at, sums, 0.0), axis=0, keepdims=True)
    grads[:, FEATURES : FEATURES + 1] = jnp.broadcast_to(spread[None], (grads.shape[0], 1, lanes))


def render(tile_ids, slots, exposure, incoming, target):
    slot_count = slots.shape[0]
    lanes = incoming.shape[2]
    smem = pl.BlockSpec(memory_space=pltpu.SMEM)
    vmem = pl.BlockSpec(memory_space=pltpu.VMEM)
    return pl.pallas_call(
        render_kernel,
        out_shape=(
            jax.ShapeDtypeStruct(target.shape, jnp.float32),
            jax.ShapeDtypeStruct((incoming.shape[0], FEATURES + 1, lanes), jnp.float32),
        ),
        in_specs=[smem, smem, smem, vmem, vmem],
        out_specs=(vmem, vmem),
        scratch_shapes=[
            pltpu.VMEM((slot_count, PIX, lanes), jnp.float32),
            pltpu.VMEM((slot_count, PIX, lanes), jnp.float32),
            pltpu.VMEM((slot_count, PIX, 2 * lanes), jnp.bfloat16),
            pltpu.VMEM((12, PIX), jnp.float32),
            pltpu.VMEM((2 * lanes, 2 * lanes), jnp.bfloat16),
            pltpu.VMEM((2 * lanes, 2 * lanes), jnp.bfloat16),
        ],
        compiler_params=pltpu.CompilerParams(vmem_limit_bytes=32 * 1024 * 1024),
        name="render",
    )(tile_ids, slots, exposure, incoming, target)


def padded(rows):
    return (rows + 7) // 8 * 8


def camera_rows(cameras, block_count):
    view_count = cameras.shape[0]
    shape = (view_count * block_count, 128)
    view_at = lax.broadcasted_iota(jnp.int32, shape, 0) // block_count
    entries = []
    for entry in range(16):
        value = jnp.full(shape, cameras[0, entry])
        for view in range(1, view_count):
            value = jnp.where(view_at == view, cameras[view, entry], value)
        entries.append(value)
    return entries


def parameter_rows(refs, view_count):
    block_count = refs[0].shape[1]

    def row(ref, at):
        own = [ref[block, at : at + 1] for block in range(block_count)]
        return jnp.concatenate(own * view_count, axis=0)

    def plane(ref, at):
        return jnp.concatenate([ref[at]] * view_count, axis=0)

    means, log_scales, rotations, opacity_logits, colour_coefs = refs
    return (
        [plane(means, at) for at in range(3)],
        [plane(log_scales, at) for at in range(3)],
        [row(rotations, at) for at in range(4)],
        row(opacity_logits, 0),
        [row(colour_coefs, at) for at in range(48)],
    )


def fill(rows, count, lanes):
    return rows if count == 0 else rows + [jnp.zeros((count, lanes), jnp.float32)]


def greet(view_count, scene_count, view, scene):
    barrier = pltpu.get_barrier_semaphore()
    for step in range(1, view_count):
        pl.semaphore_signal(
            barrier,
            inc=1,
            device_id=(lax.rem(view + step, view_count), scene),
            device_id_type=pl.DeviceIdType.MESH,
        )

    def to_scene(step, unused):
        pl.semaphore_signal(
            barrier,
            inc=1,
            device_id=(view, lax.rem(scene + step, scene_count)),
            device_id_type=pl.DeviceIdType.MESH,
        )
        return unused

    lax.fori_loop(1, scene_count, to_scene, 0)
    return barrier


def view_copy(outbox, inbox, sems, step, view, scene, view_count):
    peer = lax.rem(view + step, view_count)
    return pltpu.make_async_remote_copy(
        src_ref=outbox.at[peer],
        dst_ref=inbox.at[view],
        send_sem=sems[0].at[step],
        recv_sem=sems[1].at[step],
        device_id=(peer, scene),
        device_id_type=pl.DeviceIdType.MESH,
    )


def scene_copy(outbox, inbox, sems, step, view, scene, scene_count):
    peer = lax.rem(scene + step, scene_count)
    return pltpu.make_async_remote_copy(
        src_ref=outbox.at[peer],
        dst_ref=inbox.at[scene],
        send_sem=sems[0].at[step],
        recv_sem=sems[1].at[step],
        device_id=(view, peer),
        device_id_type=pl.DeviceIdType.MESH,
    )


def spread_kernel(
    view_count,
    scene_count,
    cameras,
    send,
    means,
    log_scales,
    rotations,
    opacity_logits,
    colour_coefs,
    incoming,
    view_out,
    view_in,
    blocks,
    scene_out,
    scene_in,
    view_send,
    view_recv,
    scene_send,
    scene_recv,
):
    view, scene = lax.axis_index("view"), lax.axis_index("scene")
    capacity = send.shape[0]
    block_count, lanes = means.shape[1], means.shape[2]
    barrier = greet(view_count, scene_count, view, scene)
    rows = project(
        camera_rows(cameras, block_count),
        *parameter_rows((means, log_scales, rotations, opacity_logits, colour_coefs), view_count),
    )
    for target in range(view_count):
        parts = []
        for block in range(block_count):
            at = target * block_count + block
            parts += [row[at : at + 1] for row in rows]
        spare = view_out.shape[1] - block_count * FEATURES
        view_out[target] = jnp.concatenate(fill(parts, spare, lanes), axis=0)
    pl.semaphore_wait(barrier, view_count + scene_count - 2)
    view_sems = (view_send, view_recv)
    for step in range(1, view_count):
        view_copy(view_out, view_in, view_sems, step, view, scene, view_count).start()
    view_in[view] = view_out[view]
    for step in range(1, view_count):
        view_copy(view_out, view_in, view_sems, step, view, scene, view_count).wait()
    for source in range(view_count):
        for block in range(block_count):
            blocks[source * block_count + block] = view_in[
                source, block * FEATURES : (block + 1) * FEATURES
            ]
    spare = scene_out.shape[1] - capacity * FEATURES

    def choose(peer, unused):
        parts = [blocks[jnp.maximum(send[at, peer], 0)] for at in range(capacity)]
        scene_out[peer] = jnp.concatenate(fill(parts, spare, lanes), axis=0)
        return unused

    def start(step, unused):
        choose(lax.rem(scene + step, scene_count), 0)
        scene_copy(scene_out, scene_in, scene_sems, step, view, scene, scene_count).start()
        return unused

    def place(source, box):
        for at in range(capacity):
            incoming[source * capacity + at] = box[at * FEATURES : (at + 1) * FEATURES]

    def finish(step, unused):
        scene_copy(scene_out, scene_in, scene_sems, step, view, scene, scene_count).wait()
        source = lax.rem(scene - step + scene_count, scene_count)
        place(source, scene_in[source])
        return unused

    scene_sems = (scene_send, scene_recv)
    lax.fori_loop(1, scene_count, start, 0)
    choose(scene, 0)
    place(scene, scene_out[scene])
    lax.fori_loop(1, scene_count, finish, 0)


def collect_kernel(
    view_count,
    scene_count,
    block_count,
    send,
    grads,
    own_grads,
    expo,
    scene_out,
    scene_in,
    view_out,
    view_in,
    scene_send,
    scene_recv,
    view_send,
    view_recv,
):
    view, scene = lax.axis_index("view"), lax.axis_index("scene")
    capacity = send.shape[0]
    lanes = grads.shape[2]
    barrier = greet(view_count, scene_count, view, scene)
    used = capacity * FEATURES
    spare = scene_out.shape[1] - used - 1

    def pack(peer, unused):
        parts = [grads[peer * capacity + at, 0:FEATURES] for at in range(capacity)]
        parts.append(grads[peer * capacity, FEATURES : FEATURES + 1])
        scene_out[peer] = jnp.concatenate(fill(parts, spare, lanes), axis=0)
        return unused

    lax.fori_loop(0, scene_count, pack, 0)
    pl.semaphore_wait(barrier, view_count + scene_count - 2)
    scene_sems = (scene_send, scene_recv)

    def start(step, unused):
        scene_copy(scene_out, scene_in, scene_sems, step, view, scene, scene_count).start()
        return unused

    def add(source, box, sums):
        sums = list(sums)
        for at in range(capacity):
            part = box[at * FEATURES : (at + 1) * FEATURES]
            home = send[at, source]
            for block in range(view_count * block_count):
                sums[block] = sums[block] + jnp.where(home == block, part, 0.0)
        sums[-1] = sums[-1] + box[used : used + 1]
        return tuple(sums)

    def finish(step, sums):
        scene_copy(scene_out, scene_in, scene_sems, step, view, scene, scene_count).wait()
        source = lax.rem(scene - step + scene_count, scene_count)
        return add(source, scene_in[source], sums)

    lax.fori_loop(1, scene_count, start, 0)
    empty = jnp.zeros((FEATURES, lanes), jnp.float32)
    sums = (empty,) * (view_count * block_count) + (jnp.zeros((1, lanes), jnp.float32),)
    sums = add(scene, scene_out[scene], sums)
    sums = lax.fori_loop(1, scene_count, finish, sums)
    expo[...] = sums[-1]
    spare = view_out.shape[1] - block_count * FEATURES
    for target in range(view_count):
        parts = list(sums[target * block_count : (target + 1) * block_count])
        view_out[target] = jnp.concatenate(fill(parts, spare, lanes), axis=0)
    view_sems = (view_send, view_recv)
    for step in range(1, view_count):
        view_copy(view_out, view_in, view_sems, step, view, scene, view_count).start()
    own_grads[view] = view_out[view]
    for step in range(1, view_count):
        view_copy(view_out, view_in, view_sems, step, view, scene, view_count).wait()
        source = lax.rem(view - step + view_count, view_count)
        own_grads[source] = view_in[source]


def unproject_kernel(
    cameras,
    own_grads,
    expo,
    means,
    log_scales,
    rotations,
    opacity_logits,
    colour_coefs,
    grad_means,
    grad_log_scales,
    grad_rotations,
    grad_opacity,
    grad_colour,
    grad_expo,
):
    view_count = cameras.shape[0]
    block_count = means.shape[1]
    cotangent = [
        jnp.concatenate(
            [
                own_grads[view, block * FEATURES + at : block * FEATURES + at + 1]
                for view in range(view_count)
                for block in range(block_count)
            ],
            axis=0,
        )
        for at in range(FEATURES)
    ]
    camera = camera_rows(cameras, block_count)
    pieces = parameter_rows(
        (means, log_scales, rotations, opacity_logits, colour_coefs), view_count
    )
    unproject = jax.vjp(functools.partial(project, camera), *pieces)[1]
    parts = unproject(cotangent)

    def over_views(value):
        total = value[0:block_count]
        for view in range(1, view_count):
            total = total + value[view * block_count : (view + 1) * block_count]
        return total

    def store(ref, at, value):
        total = over_views(value)
        for block in range(block_count):
            ref[block, at : at + 1] = total[block : block + 1]

    for at in range(3):
        grad_means[at] = over_views(parts[0][at])
        grad_log_scales[at] = over_views(parts[1][at])
    for at in range(4):
        store(grad_rotations, at, parts[2][at])
    store(grad_opacity, 0, parts[3])
    for at in range(48):
        store(grad_colour, at, parts[4][at])
    grad_expo[...] = expo[:, 0:12]


def local(
    means,
    log_scales,
    rotations,
    opacity_logits,
    colour_coefs,
    cameras,
    exposure,
    target,
    tile_ids,
    send_list,
    pair_slots,
):
    view_count = lax.axis_size("view")
    scene_count = lax.axis_size("scene")
    own_params = (
        jnp.transpose(means, (1, 0, 2)),
        jnp.transpose(log_scales, (1, 0, 2)),
        rotations,
        opacity_logits,
        colour_coefs,
    )
    block_count, lanes = means.shape[0], means.shape[2]
    capacity = send_list.shape[3]
    slots = scene_count * capacity
    send = send_list[0, 0].T
    smem = pl.BlockSpec(memory_space=pltpu.SMEM)
    vmem = pl.BlockSpec(memory_space=pltpu.VMEM)
    view_box = (view_count, padded(block_count * FEATURES), lanes)
    scene_box = (scene_count, padded(capacity * FEATURES + 1), lanes)
    limit = 32 * 1024 * 1024
    incoming = pl.pallas_call(
        functools.partial(spread_kernel, view_count, scene_count),
        out_shape=jax.ShapeDtypeStruct((slots, FEATURES, lanes), jnp.float32),
        in_specs=[smem, smem] + [vmem] * 5,
        out_specs=vmem,
        scratch_shapes=[
            pltpu.VMEM(view_box, jnp.float32),
            pltpu.VMEM(view_box, jnp.float32),
            pltpu.VMEM((view_count * block_count, FEATURES, lanes), jnp.float32),
            pltpu.VMEM(scene_box, jnp.float32),
            pltpu.VMEM(scene_box, jnp.float32),
            pltpu.SemaphoreType.DMA((view_count,)),
            pltpu.SemaphoreType.DMA((view_count,)),
            pltpu.SemaphoreType.DMA((scene_count,)),
            pltpu.SemaphoreType.DMA((scene_count,)),
        ],
        compiler_params=pltpu.CompilerParams(
            collective_id=0, has_side_effects=True, vmem_limit_bytes=limit
        ),
        name="spread",
    )(cameras, send, *own_params)
    shown, grads = render(
        tile_ids, pair_slots[0].T, exposure, incoming, jnp.transpose(target[0], (1, 0, 2))
    )
    own_grads, expo = pl.pallas_call(
        functools.partial(collect_kernel, view_count, scene_count, block_count),
        out_shape=(
            jax.ShapeDtypeStruct(view_box, jnp.float32),
            jax.ShapeDtypeStruct((1, lanes), jnp.float32),
        ),
        in_specs=[smem, vmem],
        out_specs=(vmem, vmem),
        scratch_shapes=[
            pltpu.VMEM(scene_box, jnp.float32),
            pltpu.VMEM(scene_box, jnp.float32),
            pltpu.VMEM(view_box, jnp.float32),
            pltpu.VMEM(view_box, jnp.float32),
            pltpu.SemaphoreType.DMA((scene_count,)),
            pltpu.SemaphoreType.DMA((scene_count,)),
            pltpu.SemaphoreType.DMA((view_count,)),
            pltpu.SemaphoreType.DMA((view_count,)),
        ],
        compiler_params=pltpu.CompilerParams(
            collective_id=1, has_side_effects=True, vmem_limit_bytes=limit
        ),
        name="collect",
    )(send, grads)
    param_grads = pl.pallas_call(
        unproject_kernel,
        out_shape=tuple(jax.ShapeDtypeStruct(own.shape, jnp.float32) for own in own_params)
        + (jax.ShapeDtypeStruct((1, 12), jnp.float32),),
        in_specs=[smem] + [vmem] * 7,
        out_specs=(vmem,) * 6,
        compiler_params=pltpu.CompilerParams(vmem_limit_bytes=limit),
        name="unproject",
    )(cameras, own_grads, expo, *own_params)
    return (
        jnp.transpose(shown, (1, 0, 2))[None],
        jnp.transpose(param_grads[0], (1, 0, 2)),
        jnp.transpose(param_grads[1], (1, 0, 2)),
    ) + tuple(param_grads[2:])


def solution(mesh):
    return jax.shard_map(
        local,
        mesh=mesh,
        in_specs=(
            P(("view", "scene"), None, None),
            P(("view", "scene"), None, None),
            P(("view", "scene"), None, None),
            P(("view", "scene"), None, None),
            P(("view", "scene"), None, None),
            P(),
            P("view", None),
            P("view", "scene", None, None),
            P("view", "scene"),
            P("view", "scene", None, None),
            P("view", "scene", None),
        ),
        out_specs=(
            P("view", "scene", None, None),
            P(("view", "scene"), None, None),
            P(("view", "scene"), None, None),
            P(("view", "scene"), None, None),
            P(("view", "scene"), None, None),
            P(("view", "scene"), None, None),
            P("view", None),
        ),
        check_vma=False,
    )
```

```python
import functools

import jax
import jax.numpy as jnp
from jax import lax
from jax.experimental import pallas as pl
from jax.experimental.pallas import tpu as pltpu
from jax.sharding import PartitionSpec as P

PIX = 256
TILE_COLS = 32

FEATURES = 9

SH_ZERO = 0.28209479177387814
SH_ONE = 0.4886025119029199
SH_TWO = (
    1.0925484305920792,
    -1.0925484305920792,
    0.31539156525252005,
    -1.0925484305920792,
    0.5462742152960396,
)
SH_THREE = (
    -0.5900435899266435,
    2.890611442640554,
    -0.4570457994644658,
    0.3731763325901154,
    -0.4570457994644658,
    1.445305721320277,
    -0.5900435899266435,
)


def harmonics(dir_x, dir_y, dir_z):
    sq_x, sq_y, sq_z = (dir_x * dir_x, dir_y * dir_y, dir_z * dir_z)
    sh_basis = [
        SH_ZERO * jnp.ones_like(dir_x),
        -SH_ONE * dir_y,
        SH_ONE * dir_z,
        -SH_ONE * dir_x,
        SH_TWO[0] * dir_x * dir_y,
        SH_TWO[1] * dir_y * dir_z,
        SH_TWO[2] * (2.0 * sq_z - sq_x - sq_y),
        SH_TWO[3] * dir_x * dir_z,
        SH_TWO[4] * (sq_x - sq_y),
        SH_THREE[0] * dir_y * (3.0 * sq_x - sq_y),
        SH_THREE[1] * dir_x * dir_y * dir_z,
        SH_THREE[2] * dir_y * (4.0 * sq_z - sq_x - sq_y),
        SH_THREE[3] * dir_z * (2.0 * sq_z - 3.0 * sq_x - 3.0 * sq_y),
        SH_THREE[4] * dir_x * (4.0 * sq_z - sq_x - sq_y),
        SH_THREE[5] * dir_z * (sq_x - sq_y),
        SH_THREE[6] * dir_x * (sq_x - 3.0 * sq_y),
    ]
    return sh_basis


def project(camera, position, log_scales, rotations, opacity_logits, colour_coefs):
    rotation = [camera[0:3], camera[3:6], camera[6:9]]
    translation = camera[9:12]
    focal_x, focal_y, centre_x, centre_y = camera[12:16]
    view_pos = [
        rotation[row_at][0] * position[0]
        + rotation[row_at][1] * position[1]
        + rotation[row_at][2] * position[2]
        + translation[row_at]
        for row_at in range(3)
    ]
    inv_depth = 1.0 / view_pos[2]
    quat_w = rotations[0] + 3.0
    quat_x, quat_y, quat_z = (rotations[1], rotations[2], rotations[3])
    quat_norm = jnp.sqrt(quat_w * quat_w + quat_x * quat_x + quat_y * quat_y + quat_z * quat_z)
    quat_w, quat_x, quat_y, quat_z = (
        quat_w / quat_norm,
        quat_x / quat_norm,
        quat_y / quat_norm,
        quat_z / quat_norm,
    )
    spin_matrix = [
        [
            1.0 - 2.0 * (quat_y * quat_y + quat_z * quat_z),
            2.0 * (quat_x * quat_y - quat_w * quat_z),
            2.0 * (quat_x * quat_z + quat_w * quat_y),
        ],
        [
            2.0 * (quat_x * quat_y + quat_w * quat_z),
            1.0 - 2.0 * (quat_x * quat_x + quat_z * quat_z),
            2.0 * (quat_y * quat_z - quat_w * quat_x),
        ],
        [
            2.0 * (quat_x * quat_z - quat_w * quat_y),
            2.0 * (quat_y * quat_z + quat_w * quat_x),
            1.0 - 2.0 * (quat_x * quat_x + quat_y * quat_y),
        ],
    ]
    scales = [jnp.exp(row) for row in log_scales]
    world_frame = [
        [spin_matrix[row_at][col_at] * scales[col_at] for col_at in range(3)]
        for row_at in range(3)
    ]
    jacobian = [
        [
            focal_x * inv_depth * rotation[0][col_at]
            - focal_x * view_pos[0] * inv_depth * inv_depth * rotation[2][col_at]
            for col_at in range(3)
        ],
        [
            focal_y * inv_depth * rotation[1][col_at]
            - focal_y * view_pos[1] * inv_depth * inv_depth * rotation[2][col_at]
            for col_at in range(3)
        ],
    ]
    screen_frame = [
        [
            jacobian[row_at][0] * world_frame[0][col_at]
            + jacobian[row_at][1] * world_frame[1][col_at]
            + jacobian[row_at][2] * world_frame[2][col_at]
            for col_at in range(3)
        ]
        for row_at in range(2)
    ]
    sigma_xx = screen_frame[0][0] ** 2 + screen_frame[0][1] ** 2 + screen_frame[0][2] ** 2 + 0.3
    sigma_yy = screen_frame[1][0] ** 2 + screen_frame[1][1] ** 2 + screen_frame[1][2] ** 2 + 0.3
    sigma_xy = (
        screen_frame[0][0] * screen_frame[1][0]
        + screen_frame[0][1] * screen_frame[1][1]
        + screen_frame[0][2] * screen_frame[1][2]
    )
    determinant = sigma_xx * sigma_yy - sigma_xy * sigma_xy
    screen_x = focal_x * view_pos[0] * inv_depth + centre_x
    screen_y = focal_y * view_pos[1] * inv_depth + centre_y
    opacity = jax.nn.sigmoid(opacity_logits)
    eye_pos = [
        -(
            rotation[0][col_at] * translation[0]
            + rotation[1][col_at] * translation[1]
            + rotation[2][col_at] * translation[2]
        )
        for col_at in range(3)
    ]
    offsets = [position[col_at] - eye_pos[col_at] for col_at in range(3)]
    eye_dist = jnp.sqrt(offsets[0] ** 2 + offsets[1] ** 2 + offsets[2] ** 2)
    sh_basis = harmonics(offsets[0] / eye_dist, offsets[1] / eye_dist, offsets[2] / eye_dist)
    colour = []
    for channel in range(3):
        total = sh_basis[0] * colour_coefs[channel]
        for order in range(1, 16):
            total = total + sh_basis[order] * colour_coefs[3 * order + channel]
        colour.append(jnp.maximum(0.5 + total, 0.0))
    return [
        screen_x,
        screen_y,
        sigma_yy / determinant,
        -sigma_xy / determinant,
        sigma_xx / determinant,
        opacity,
    ] + colour


LOG2E = 1.4426950408889634


def split_pair(values):
    high = values.astype(jnp.bfloat16)
    low = (values - high.astype(jnp.float32)).astype(jnp.bfloat16)
    return jnp.concatenate([high, low], axis=1)


def render_kernel(
    tile_ids,
    slots,
    exposure,
    incoming,
    target,
    shown,
    grads,
    weight,
    ratio,
    weight_pair,
    expo_sum,
    before_mat,
    after_mat,
):
    slot_count, tile_count = slots.shape
    lanes = incoming.shape[2]
    row_at = lax.broadcasted_iota(jnp.int32, (2 * lanes, 2 * lanes), 0) % lanes
    col_at = lax.broadcasted_iota(jnp.int32, (2 * lanes, 2 * lanes), 1)
    total = col_at >= lanes
    before_mat[...] = jnp.where(total | (row_at < col_at), 1.0, 0.0).astype(jnp.bfloat16)
    after_mat[...] = jnp.where(total | (row_at > col_at), 1.0, 0.0).astype(jnp.bfloat16)
    grads[...] = jnp.zeros_like(grads)
    expo_sum[...] = jnp.zeros_like(expo_sum)
    mixing = [
        [exposure[0, 3 * i + j] + (1.0 if i == j else 0.0) for j in range(3)] for i in range(3)
    ]
    offset = [exposure[0, 9 + i] for i in range(3)]
    local_x = [
        lax.broadcasted_iota(jnp.int32, (8, lanes), 0).astype(jnp.float32) + (8.0 * half - 7.5)
        for half in range(2)
    ]
    zero_rows = jnp.zeros((2, lanes), jnp.float32)

    def load(tile, at, centre_x, centre_y):
        block = incoming[slots[at, tile]]
        rows = [block[i : i + 1] for i in range(FEATURES)]
        rows[0] = rows[0] - centre_x
        rows[1] = rows[1] - centre_y
        return rows, block[6:9]

    def colour_side(tile, at):
        colour = incoming[slots[at, tile]][6:9]
        high = colour.astype(jnp.bfloat16).astype(jnp.float32)
        return jnp.concatenate(
            [high, colour - high, high, jnp.zeros((7, lanes), jnp.float32)], axis=0
        ).astype(jnp.bfloat16)

    def moments(heat):
        flat, tilt, bend = [], [], []
        for half in range(2):
            sums = None
            for line in range(PIX // 32):
                far = PIX // 16 - 1 - line
                first = heat[16 * line + 8 * half : 16 * line + 8 * half + 8]
                last = heat[16 * far + 8 * half : 16 * far + 8 * half + 8]
                both, apart = last + first, last - first
                side = far - 7.5
                terms = (both, apart * side, both * (side * side))
                sums = terms if sums is None else [a + b for a, b in zip(sums, terms)]
            flat.append(sums[0])
            tilt.append(sums[1])
            bend.append(sums[2])
        slide = [part * side for part, side in zip(flat, local_x)]
        fields = [
            flat[0] + flat[1],
            slide[0] + slide[1],
            tilt[0] + tilt[1],
            slide[0] * local_x[0] + slide[1] * local_x[1],
            tilt[0] * local_x[0] + tilt[1] * local_x[1],
            bend[0] + bend[1],
        ]
        return [jnp.sum(field, axis=0, keepdims=True) for field in fields]

    def one_tile(tile, live):
        tile_id = tile_ids[0, tile]
        centre_x = (16 * (tile_id % TILE_COLS) + 8).astype(jnp.float32)
        centre_y = (16 * (tile_id // TILE_COLS) + 8).astype(jnp.float32)
        carry = None
        shade = None
        for at in range(live):
            rows, colour = load(tile, at, centre_x, centre_y)
            wide = [jnp.broadcast_to(row, (8, lanes)) for row in rows[:6]]
            gap_x = [side - wide[0] for side in local_x]
            scaled_a = wide[2] * (-0.5 * LOG2E)
            scaled_b = wide[3] * (-LOG2E)
            scaled_c = wide[4] * (-0.5 * LOG2E)
            part_x = [scaled_a * gap * gap for gap in gap_x]
            pieces = []
            for line in range(PIX // 16):
                gap_y = (line - 7.5) - wide[1]
                part_y = scaled_c * gap_y * gap_y
                slope = scaled_b * gap_y
                for half in range(2):
                    pieces.append(
                        wide[5] * jnp.exp2(part_x[half] + gap_x[half] * slope + part_y)
                    )
            alpha = jnp.concatenate(pieces, axis=0)
            log_keep = jnp.log(1.0 - alpha)
            width = 2 * lanes if at + 1 < live else lanes
            sums = jnp.dot(
                split_pair(log_keep), before_mat[:, :width], preferred_element_type=jnp.float32
            )
            inside = sums[:, :lanes]
            if at > 0:
                inside = inside + carry
            if at + 1 < live:
                carry = sums[:, lanes:] if at == 0 else carry + sums[:, lanes:]
            seen = alpha * jnp.exp(inside)
            pair = split_pair(seen)
            weight[at] = seen
            ratio[at] = alpha * jnp.exp(-log_keep)
            weight_pair[at] = pair
            high = colour.astype(jnp.bfloat16).astype(jnp.float32)
            low = colour - high
            left = jnp.concatenate([high, low, zero_rows], axis=0)
            right = jnp.concatenate([high, jnp.zeros((5, lanes), jnp.float32)], axis=0)
            mixed = jnp.concatenate([left, right], axis=1).astype(jnp.bfloat16)
            term = lax.dot_general(
                mixed, pair, (((1,), (1,)), ((), ())), preferred_element_type=jnp.float32
            )
            shade = term if at == 0 else shade + term
        tone = [shade[i : i + 1] + shade[i + 3 : i + 4] for i in range(3)]
        image = [
            mixing[i][0] * tone[0] + mixing[i][1] * tone[1] + mixing[i][2] * tone[2] + offset[i]
            for i in range(3)
        ]
        for i in range(3):
            shown[i, pl.ds(tile, 1)] = image[i]
        miss = [image[i] - target[i, pl.ds(tile, 1)] for i in range(3)]
        expo_sum[...] += jnp.concatenate(
            [miss[i] * tone[j] for i in range(3) for j in range(3)] + miss, axis=0
        )
        back = jnp.concatenate(
            [
                mixing[0][j] * miss[0] + mixing[1][j] * miss[1] + mixing[2][j] * miss[2]
                for j in range(3)
            ],
            axis=0,
        )
        back_high = back.astype(jnp.bfloat16).astype(jnp.float32)
        back_low = back - back_high
        back_left = jnp.concatenate(
            [back_high, back_low, jnp.zeros((2, PIX), jnp.float32)], axis=0
        ).astype(jnp.bfloat16)
        back_side = jnp.transpose(
            jnp.concatenate(
                [back_high, back_high, back_low, jnp.zeros((7, PIX), jnp.float32)], axis=0
            )
        ).astype(jnp.bfloat16)
        pulls = []
        for first in range(0, live, 2):
            sides = [colour_side(tile, at) for at in range(first, min(first + 2, live))]
            both = jnp.dot(
                back_side, jnp.concatenate(sides, axis=1), preferred_element_type=jnp.float32
            )
            pulls += [both[:, at * lanes : (at + 1) * lanes] for at in range(len(sides))]
        carry = None
        for at in reversed(range(live)):
            rows, colour = load(tile, at, centre_x, centre_y)
            gain = weight[at] * pulls[at]
            width = 2 * lanes if at > 0 else lanes
            sums = jnp.dot(
                split_pair(gain), after_mat[:, :width], preferred_element_type=jnp.float32
            )
            behind = sums[:, :lanes]
            if at + 1 < live:
                behind = behind + carry
            if at > 0:
                carry = sums[:, lanes:] if at + 1 == live else carry + sums[:, lanes:]
            heat = gain - behind * ratio[at]
            tint = jnp.dot(back_left, weight_pair[at], preferred_element_type=jnp.float32)
            tint = tint[:, :lanes] + tint[:, lanes:]
            tint = tint[0:3] + tint[3:6]
            pos_x, pos_y, con_a, con_b, con_c, opacity = rows[:6]
            m_one, m_x, m_y, m_xx, m_xy, m_yy = moments(heat)
            d_x = m_x - pos_x * m_one
            d_y = m_y - pos_y * m_one
            d_xx = m_xx - pos_x * (m_x + d_x)
            d_xy = m_xy - pos_x * m_y - pos_y * d_x
            d_yy = m_yy - pos_y * (m_y + d_y)
            grads[slots[at, tile], 0:FEATURES] += jnp.concatenate(
                [
                    con_a * d_x + con_b * d_y,
                    con_b * d_x + con_c * d_y,
                    -0.5 * d_xx,
                    -d_xy,
                    -0.5 * d_yy,
                    m_one / opacity,
                    tint,
                ],
                axis=0,
            )

    def tile_step(tile, unused):
        live = jnp.int32(0)
        for at in range(slot_count):
            live = live + jnp.where(slots[at, tile] >= 0, 1, 0)
        for number in range(1, slot_count + 1):
            pl.when(live == number)(functools.partial(one_tile, tile, number))
        return unused

    lax.fori_loop(0, tile_count, tile_step, 0)
    sums = jnp.sum(expo_sum[...], axis=1, keepdims=True)
    lane_at = lax.broadcasted_iota(jnp.int32, (12, lanes), 1)
    row_at = lax.broadcasted_iota(jnp.int32, (12, lanes), 0)
    spread = jnp.sum(jnp.where(lane_at == row_at, sums, 0.0), axis=0, keepdims=True)
    grads[:, FEATURES : FEATURES + 1] = jnp.broadcast_to(spread[None], (grads.shape[0], 1, lanes))


def render(tile_ids, slots, exposure, incoming, target):
    slot_count = slots.shape[0]
    lanes = incoming.shape[2]
    smem = pl.BlockSpec(memory_space=pltpu.SMEM)
    vmem = pl.BlockSpec(memory_space=pltpu.VMEM)
    return pl.pallas_call(
        render_kernel,
        out_shape=(
            jax.ShapeDtypeStruct(target.shape, jnp.float32),
            jax.ShapeDtypeStruct((incoming.shape[0], FEATURES + 1, lanes), jnp.float32),
        ),
        in_specs=[smem, smem, smem, vmem, vmem],
        out_specs=(vmem, vmem),
        scratch_shapes=[
            pltpu.VMEM((slot_count, PIX, lanes), jnp.float32),
            pltpu.VMEM((slot_count, PIX, lanes), jnp.float32),
            pltpu.VMEM((slot_count, PIX, 2 * lanes), jnp.bfloat16),
            pltpu.VMEM((12, PIX), jnp.float32),
            pltpu.VMEM((2 * lanes, 2 * lanes), jnp.bfloat16),
            pltpu.VMEM((2 * lanes, 2 * lanes), jnp.bfloat16),
        ],
        compiler_params=pltpu.CompilerParams(vmem_limit_bytes=32 * 1024 * 1024),
        name="render",
    )(tile_ids, slots, exposure, incoming, target)


def padded(rows):
    return (rows + 7) // 8 * 8


def camera_rows(cameras, block_count):
    view_count = cameras.shape[0]
    shape = (view_count * block_count, 128)
    view_at = lax.broadcasted_iota(jnp.int32, shape, 0) // block_count
    entries = []
    for entry in range(16):
        value = jnp.full(shape, cameras[0, entry])
        for view in range(1, view_count):
            value = jnp.where(view_at == view, cameras[view, entry], value)
        entries.append(value)
    return entries


def parameter_rows(refs, view_count):
    block_count = refs[0].shape[1]

    def row(ref, at):
        own = [ref[block, at : at + 1] for block in range(block_count)]
        return jnp.concatenate(own * view_count, axis=0)

    def plane(ref, at):
        return jnp.concatenate([ref[at]] * view_count, axis=0)

    means, log_scales, rotations, opacity_logits, colour_coefs = refs
    return (
        [plane(means, at) for at in range(3)],
        [plane(log_scales, at) for at in range(3)],
        [row(rotations, at) for at in range(4)],
        row(opacity_logits, 0),
        [row(colour_coefs, at) for at in range(48)],
    )


def fill(rows, count, lanes):
    return rows if count == 0 else rows + [jnp.zeros((count, lanes), jnp.float32)]


def greet(view_count, scene_count, view, scene):
    barrier = pltpu.get_barrier_semaphore()
    for step in range(1, view_count):
        pl.semaphore_signal(
            barrier,
            inc=1,
            device_id=(lax.rem(view + step, view_count), scene),
            device_id_type=pl.DeviceIdType.MESH,
        )

    def to_scene(step, unused):
        pl.semaphore_signal(
            barrier,
            inc=1,
            device_id=(view, lax.rem(scene + step, scene_count)),
            device_id_type=pl.DeviceIdType.MESH,
        )
        return unused

    lax.fori_loop(1, scene_count, to_scene, 0)
    return barrier


def view_copy(outbox, inbox, sems, step, view, scene, view_count):
    peer = lax.rem(view + step, view_count)
    return pltpu.make_async_remote_copy(
        src_ref=outbox.at[peer],
        dst_ref=inbox.at[view],
        send_sem=sems[0].at[step],
        recv_sem=sems[1].at[step],
        device_id=(peer, scene),
        device_id_type=pl.DeviceIdType.MESH,
    )


def scene_copy(outbox, inbox, sems, step, view, scene, scene_count):
    peer = lax.rem(scene + step, scene_count)
    return pltpu.make_async_remote_copy(
        src_ref=outbox.at[peer],
        dst_ref=inbox.at[scene],
        send_sem=sems[0].at[step],
        recv_sem=sems[1].at[step],
        device_id=(view, peer),
        device_id_type=pl.DeviceIdType.MESH,
    )


def spread_kernel(
    view_count,
    scene_count,
    cameras,
    send,
    means,
    log_scales,
    rotations,
    opacity_logits,
    colour_coefs,
    incoming,
    view_out,
    view_in,
    blocks,
    scene_out,
    scene_in,
    view_send,
    view_recv,
    scene_send,
    scene_recv,
):
    view, scene = lax.axis_index("view"), lax.axis_index("scene")
    capacity = send.shape[0]
    block_count, lanes = means.shape[1], means.shape[2]
    barrier = greet(view_count, scene_count, view, scene)
    rows = project(
        camera_rows(cameras, block_count),
        *parameter_rows((means, log_scales, rotations, opacity_logits, colour_coefs), view_count),
    )
    for target in range(view_count):
        parts = []
        for block in range(block_count):
            at = target * block_count + block
            parts += [row[at : at + 1] for row in rows]
        spare = view_out.shape[1] - block_count * FEATURES
        view_out[target] = jnp.concatenate(fill(parts, spare, lanes), axis=0)
    pl.semaphore_wait(barrier, view_count + scene_count - 2)
    view_sems = (view_send, view_recv)
    for step in range(1, view_count):
        view_copy(view_out, view_in, view_sems, step, view, scene, view_count).start()
    view_in[view] = view_out[view]
    for step in range(1, view_count):
        view_copy(view_out, view_in, view_sems, step, view, scene, view_count).wait()
    for source in range(view_count):
        for block in range(block_count):
            blocks[source * block_count + block] = view_in[
                source, block * FEATURES : (block + 1) * FEATURES
            ]
    spare = scene_out.shape[1] - capacity * FEATURES

    def choose(peer, unused):
        parts = [blocks[jnp.maximum(send[at, peer], 0)] for at in range(capacity)]
        scene_out[peer] = jnp.concatenate(fill(parts, spare, lanes), axis=0)
        return unused

    def start(step, unused):
        choose(lax.rem(scene + step, scene_count), 0)
        scene_copy(scene_out, scene_in, scene_sems, step, view, scene, scene_count).start()
        return unused

    def place(source, box):
        for at in range(capacity):
            incoming[source * capacity + at] = box[at * FEATURES : (at + 1) * FEATURES]

    def finish(step, unused):
        scene_copy(scene_out, scene_in, scene_sems, step, view, scene, scene_count).wait()
        source = lax.rem(scene - step + scene_count, scene_count)
        place(source, scene_in[source])
        return unused

    scene_sems = (scene_send, scene_recv)
    lax.fori_loop(1, scene_count, start, 0)
    choose(scene, 0)
    place(scene, scene_out[scene])
    lax.fori_loop(1, scene_count, finish, 0)


def collect_kernel(
    view_count,
    scene_count,
    block_count,
    send,
    grads,
    own_grads,
    expo,
    scene_out,
    scene_in,
    view_out,
    view_in,
    scene_send,
    scene_recv,
    view_send,
    view_recv,
):
    view, scene = lax.axis_index("view"), lax.axis_index("scene")
    capacity = send.shape[0]
    lanes = grads.shape[2]
    barrier = greet(view_count, scene_count, view, scene)
    used = capacity * FEATURES
    spare = scene_out.shape[1] - used - 1

    def pack(peer, unused):
        parts = [grads[peer * capacity + at, 0:FEATURES] for at in range(capacity)]
        parts.append(grads[peer * capacity, FEATURES : FEATURES + 1])
        scene_out[peer] = jnp.concatenate(fill(parts, spare, lanes), axis=0)
        return unused

    lax.fori_loop(0, scene_count, pack, 0)
    pl.semaphore_wait(barrier, view_count + scene_count - 2)
    scene_sems = (scene_send, scene_recv)

    def start(step, unused):
        scene_copy(scene_out, scene_in, scene_sems, step, view, scene, scene_count).start()
        return unused

    def add(source, box, sums):
        sums = list(sums)
        for at in range(capacity):
            part = box[at * FEATURES : (at + 1) * FEATURES]
            home = send[at, source]
            for block in range(view_count * block_count):
                sums[block] = sums[block] + jnp.where(home == block, part, 0.0)
        sums[-1] = sums[-1] + box[used : used + 1]
        return tuple(sums)

    def finish(step, sums):
        scene_copy(scene_out, scene_in, scene_sems, step, view, scene, scene_count).wait()
        source = lax.rem(scene - step + scene_count, scene_count)
        return add(source, scene_in[source], sums)

    lax.fori_loop(1, scene_count, start, 0)
    empty = jnp.zeros((FEATURES, lanes), jnp.float32)
    sums = (empty,) * (view_count * block_count) + (jnp.zeros((1, lanes), jnp.float32),)
    sums = add(scene, scene_out[scene], sums)
    sums = lax.fori_loop(1, scene_count, finish, sums)
    expo[...] = sums[-1]
    spare = view_out.shape[1] - block_count * FEATURES
    for target in range(view_count):
        parts = list(sums[target * block_count : (target + 1) * block_count])
        view_out[target] = jnp.concatenate(fill(parts, spare, lanes), axis=0)
    view_sems = (view_send, view_recv)
    for step in range(1, view_count):
        view_copy(view_out, view_in, view_sems, step, view, scene, view_count).start()
    own_grads[view] = view_out[view]
    for step in range(1, view_count):
        view_copy(view_out, view_in, view_sems, step, view, scene, view_count).wait()
        source = lax.rem(view - step + view_count, view_count)
        own_grads[source] = view_in[source]


def unproject_kernel(
    cameras,
    own_grads,
    expo,
    means,
    log_scales,
    rotations,
    opacity_logits,
    colour_coefs,
    grad_means,
    grad_log_scales,
    grad_rotations,
    grad_opacity,
    grad_colour,
    grad_expo,
):
    view_count = cameras.shape[0]
    block_count = means.shape[1]
    cotangent = [
        jnp.concatenate(
            [
                own_grads[view, block * FEATURES + at : block * FEATURES + at + 1]
                for view in range(view_count)
                for block in range(block_count)
            ],
            axis=0,
        )
        for at in range(FEATURES)
    ]
    camera = camera_rows(cameras, block_count)
    pieces = parameter_rows(
        (means, log_scales, rotations, opacity_logits, colour_coefs), view_count
    )
    unproject = jax.vjp(functools.partial(project, camera), *pieces)[1]
    parts = unproject(cotangent)

    def over_views(value):
        total = value[0:block_count]
        for view in range(1, view_count):
            total = total + value[view * block_count : (view + 1) * block_count]
        return total

    def store(ref, at, value):
        total = over_views(value)
        for block in range(block_count):
            ref[block, at : at + 1] = total[block : block + 1]

    for at in range(3):
        grad_means[at] = over_views(parts[0][at])
        grad_log_scales[at] = over_views(parts[1][at])
    for at in range(4):
        store(grad_rotations, at, parts[2][at])
    store(grad_opacity, 0, parts[3])
    for at in range(48):
        store(grad_colour, at, parts[4][at])
    grad_expo[...] = expo[:, 0:12]


def local(
    means,
    log_scales,
    rotations,
    opacity_logits,
    colour_coefs,
    cameras,
    exposure,
    target,
    tile_ids,
    send_list,
    pair_slots,
):
    view_count = lax.axis_size("view")
    scene_count = lax.axis_size("scene")
    own_params = (
        jnp.transpose(means, (1, 0, 2)),
        jnp.transpose(log_scales, (1, 0, 2)),
        rotations,
        opacity_logits,
        colour_coefs,
    )
    block_count, lanes = means.shape[0], means.shape[2]
    capacity = send_list.shape[3]
    slots = scene_count * capacity
    send = send_list[0, 0].T
    smem = pl.BlockSpec(memory_space=pltpu.SMEM)
    vmem = pl.BlockSpec(memory_space=pltpu.VMEM)
    view_box = (view_count, padded(block_count * FEATURES), lanes)
    scene_box = (scene_count, padded(capacity * FEATURES + 1), lanes)
    limit = 32 * 1024 * 1024
    incoming = pl.pallas_call(
        functools.partial(spread_kernel, view_count, scene_count),
        out_shape=jax.ShapeDtypeStruct((slots, FEATURES, lanes), jnp.float32),
        in_specs=[smem, smem] + [vmem] * 5,
        out_specs=vmem,
        scratch_shapes=[
            pltpu.VMEM(view_box, jnp.float32),
            pltpu.VMEM(view_box, jnp.float32),
            pltpu.VMEM((view_count * block_count, FEATURES, lanes), jnp.float32),
            pltpu.VMEM(scene_box, jnp.float32),
            pltpu.VMEM(scene_box, jnp.float32),
            pltpu.SemaphoreType.DMA((view_count,)),
            pltpu.SemaphoreType.DMA((view_count,)),
            pltpu.SemaphoreType.DMA((scene_count,)),
            pltpu.SemaphoreType.DMA((scene_count,)),
        ],
        compiler_params=pltpu.CompilerParams(
            collective_id=0, has_side_effects=True, vmem_limit_bytes=limit
        ),
        name="spread",
    )(cameras, send, *own_params)
    shown, grads = render(
        tile_ids, pair_slots[0].T, exposure, incoming, jnp.transpose(target[0], (1, 0, 2))
    )
    own_grads, expo = pl.pallas_call(
        functools.partial(collect_kernel, view_count, scene_count, block_count),
        out_shape=(
            jax.ShapeDtypeStruct(view_box, jnp.float32),
            jax.ShapeDtypeStruct((1, lanes), jnp.float32),
        ),
        in_specs=[smem, vmem],
        out_specs=(vmem, vmem),
        scratch_shapes=[
            pltpu.VMEM(scene_box, jnp.float32),
            pltpu.VMEM(scene_box, jnp.float32),
            pltpu.VMEM(view_box, jnp.float32),
            pltpu.VMEM(view_box, jnp.float32),
            pltpu.SemaphoreType.DMA((scene_count,)),
            pltpu.SemaphoreType.DMA((scene_count,)),
            pltpu.SemaphoreType.DMA((view_count,)),
            pltpu.SemaphoreType.DMA((view_count,)),
        ],
        compiler_params=pltpu.CompilerParams(
            collective_id=1, has_side_effects=True, vmem_limit_bytes=limit
        ),
        name="collect",
    )(send, grads)
    param_grads = pl.pallas_call(
        unproject_kernel,
        out_shape=tuple(jax.ShapeDtypeStruct(own.shape, jnp.float32) for own in own_params)
        + (jax.ShapeDtypeStruct((1, 12), jnp.float32),),
        in_specs=[smem] + [vmem] * 7,
        out_specs=(vmem,) * 6,
        compiler_params=pltpu.CompilerParams(vmem_limit_bytes=limit),
        name="unproject",
    )(cameras, own_grads, expo, *own_params)
    return (
        jnp.transpose(shown, (1, 0, 2))[None],
        jnp.transpose(param_grads[0], (1, 0, 2)),
        jnp.transpose(param_grads[1], (1, 0, 2)),
    ) + tuple(param_grads[2:])


def solution(mesh):
    return jax.shard_map(
        local,
        mesh=mesh,
        in_specs=(
            P(("view", "scene"), None, None),
            P(("view", "scene"), None, None),
            P(("view", "scene"), None, None),
            P(("view", "scene"), None, None),
            P(("view", "scene"), None, None),
            P(),
            P("view", None),
            P("view", "scene", None, None),
            P("view", "scene"),
            P("view", "scene", None, None),
            P("view", "scene", None),
        ),
        out_specs=(
            P("view", "scene", None, None),
            P(("view", "scene"), None, None),
            P(("view", "scene"), None, None),
            P(("view", "scene"), None, None),
            P(("view", "scene"), None, None),
            P(("view", "scene"), None, None),
            P("view", None),
        ),
        check_vma=False,
    )
```
